128 devices in a mesh: occ: 64 (over z_lo, x, y, core), aux: 2 (over z_hi).
Axes of the slice: x: 4, y: 4, z: 4 (z_hi: 2, z_lo: 2; z = z_hi * 2 + z_lo), core: 2. Of those that a mesh axis runs over, the one named last changes fastest.
Arguments:
- occ_energy: float32 [256], replicated, may hold values from -2 to -0.3
- vir_energy: float32 [512], replicated, may hold values from 0.2 to 3
- factors: bfloat16 [256, 512, 2048], P(('occ', 'aux')), may hold values from -3.5 to 3.5
Outputs:
- gamma_three: bfloat16 [256, 512, 2048], P(('occ', 'aux'))
- gamma_two: float32 [2048, 2048], P(('occ', 'aux'))
The draws below stay inside these ranges and needn't reach their ends.
All inputs are finite; a program needn't handle non-finite values.
Results may differ from the reference program's by a relative error of at most 0.0043.
Values may be sent and summed in bfloat16 or wider, within the bound.
A program may use at most 128 MiB of HBM per device.

```python
import jax
import jax.numpy as jnp
from jax import lax

OCC_DEV = 2
NVIR = 512
NAUX = 2048
ROUNDS = 1
NOCC = 256


def with_spikes(result, own_key, source, target, shards_of, factor):
    def block_of(axis_at):
        return (jnp.arange(result.shape[axis_at]) // (result.shape[axis_at] // shards_of)).reshape((-1,) + (1,) * (result.ndim - 1 - axis_at))

    one_side = jax.random.permutation(own_key, shards_of)[block_of(target)]
    second = (block_of(target) + shards_of // 2) % shards_of
    return jnp.where((block_of(source) == one_side) | (block_of(source) == second), factor * result, result)


def levels(stream_key, shape, pieces, low, top_value):
    def one(axis_at, parts):
        draws = jax.random.uniform(jax.random.fold_in(jax.random.fold_in(stream_key, 6), axis_at), (parts,), jnp.float32, low / len(pieces), top_value / len(pieces))
        return jnp.repeat(jnp.exp(draws), shape[axis_at] // parts).reshape((-1,) + (1,) * (len(shape) - axis_at - 1))

    loudness = one(*pieces[0])
    for cut in pieces[1:]:
        loudness = loudness * one(*cut)
    return loudness


def bell_draw_with(own_key, extent, spread, limit, shards, heavy, kind=jnp.bfloat16):
    values = spread * jax.random.normal(own_key, extent, jnp.float32)
    if shards:
        values = values * levels(own_key, extent, shards, -0.22, 0.18)
    return jnp.clip(with_spikes(values, jax.random.fold_in(own_key, 3), *heavy), -limit, limit).astype(kind)


def setup_inputs(seed: int = 0) -> dict:
    keys = jax.random.split(jax.random.key(seed), 4)
    return {
        "occ_energy": jnp.clip(jax.random.uniform(keys[0], (NOCC,), jnp.float32, -2.0, -0.3), -2.0, -0.3),
        "vir_energy": jnp.clip(jax.random.uniform(keys[1], (NVIR,), jnp.float32, 0.2, 3.0), 0.2, 3.0),
        "factors": bell_draw_with(keys[2], (NOCC, NVIR, NAUX), 0.15, 3.5, ((0, 128),), (0, 2, 128, 5.5)),
    }


def pair_amplitudes(left_block, right_block, left_energy, right_energy, vir_energy):
    orbitals = left_energy.shape[0]
    virtuals = vir_energy.shape[0]
    ints = lax.dot_general(left_block, right_block, (((1,), (1,)), ((), ())), preferred_element_type=jnp.float32)
    ints = ints.reshape(orbitals, virtuals, orbitals, virtuals)
    swapped = jnp.transpose(ints, (0, 3, 2, 1))
    gap = (vir_energy[None, :, None, None] + vir_energy[None, None, None, :]
           - left_energy[:, None, None, None] - right_energy[None, None, :, None])
    amps = ((2.0 * ints - swapped) / gap).astype(jnp.bfloat16)
    return amps.reshape(orbitals * virtuals, orbitals * virtuals)


def reference(occ_energy, vir_energy, factors):
    nblocks = NOCC // OCC_DEV
    width = OCC_DEV * NVIR
    blocks = factors.reshape(nblocks, width, NAUX)
    energies = occ_energy.reshape(nblocks, OCC_DEV)
    gamma_sum = jnp.zeros((nblocks, width, NAUX), jnp.float32)
    for step in range(1, ROUNDS + 1):
        partners = jnp.roll(blocks, step, axis=0)
        partner_energies = jnp.roll(energies, step, axis=0)

        def pair_work(item):
            left_block, right_block, left_energy, right_energy = item
            amps = pair_amplitudes(left_block, right_block, left_energy, right_energy, vir_energy)
            own_term = jnp.dot(amps, right_block, preferred_element_type=jnp.float32)
            partner_term = lax.dot_general(amps, left_block, (((0,), (0,)), ((), ())),
                                           preferred_element_type=jnp.float32).astype(jnp.bfloat16)
            return own_term, partner_term

        own_terms, partner_terms = lax.map(pair_work, (blocks, partners, energies, partner_energies))
        arrived = jnp.roll(partner_terms, -step, axis=0)
        gamma_sum = gamma_sum + own_terms + lax.optimization_barrier(arrived).astype(jnp.float32)
    gamma_three = gamma_sum.astype(jnp.bfloat16)
    flat_gamma = gamma_three.reshape(NOCC * NVIR, NAUX)
    flat_factors = factors.reshape(NOCC * NVIR, NAUX)
    scale = (NOCC * NVIR) ** -0.5
    gamma_two = lax.dot_general(flat_gamma, flat_factors, (((0,), (0,)), ((), ())),
                                preferred_element_type=jnp.float32) * scale
    return gamma_three.reshape(NOCC, NVIR, NAUX), gamma_two
```

```python
import jax
import jax.numpy as jnp
from jax import lax
from jax.experimental import pallas as pl
from jax.experimental.pallas import tpu as pltpu
from jax.sharding import PartitionSpec as P

MESH = pl.DeviceIdType.MESH
NT = (((1,), (1,)), ((), ()))
CHUNKS = 16
TILE = 256


def device(position):
    return (position // 2, position % 2)


def pair_kernel(
    occ, vir, factors, gamma, own, near, far, ints, amps, near_term, far_term, base,
    load_sem, near_send, near_recv, far_send, far_recv,
):
    width, panel = own.shape
    virtuals = vir.shape[1]
    chunk = width // CHUNKS
    count = 2 * lax.axis_size("occ")
    me = lax.axis_index("occ") * 2 + lax.axis_index("aux")
    even = me % 2 == 0
    step = 1 - 2 * (me % 2)
    near_block = (me + step + count) % count
    far_block = (me - step + count) % count
    onward = (me + 2 * step + count) % count
    behind = (me - 2 * step + count) % count

    load = pltpu.make_async_copy(factors, own, load_sem)
    load.start()

    barrier = pltpu.get_barrier_semaphore()
    for other in (near_block, onward, behind):
        pl.semaphore_signal(barrier, inc=1, device_id=device(other), device_id_type=MESH)
    pl.semaphore_wait(barrier, 3)

    def rows(c):
        return pl.ds(c * chunk, chunk)

    direct = [
        pltpu.make_async_remote_copy(
            src_ref=factors.at[rows(c)], dst_ref=near.at[rows(c)],
            send_sem=near_send.at[c], recv_sem=near_recv.at[c],
            device_id=device(near_block), device_id_type=MESH)
        for c in range(CHUNKS)
    ]
    passed = [
        pltpu.make_async_remote_copy(
            src_ref=near.at[rows(c)], dst_ref=far.at[rows(c)],
            send_sem=far_send.at[c], recv_sem=far_recv.at[c],
            device_id=device(onward), device_id_type=MESH)
        for c in range(CHUNKS)
    ]
    for copy in direct:
        copy.start()

    row = jnp.broadcast_to(vir[...], (virtuals, virtuals))
    base[...] = row + row.T
    load.wait()

    def pair_ints(block, which, piece):
        half = piece % 2

        @pl.loop(0, width // TILE)
        def _(r):
            at = pl.ds(pl.multiple_of(r * TILE, TILE), TILE)
            ints[which, at, half * TILE:(half + 1) * TILE] = lax.dot_general(
                own[at, :], block[piece * TILE:(piece + 1) * TILE, :], NT,
                preferred_element_type=jnp.float32)

    def pair_amps(which, other, n):
        other_energy = occ[2 * other + n]
        for i in range(2):
            energy = occ[2 * me + i]
            for a in range(virtuals // TILE):
                for b in range(virtuals // TILE):
                    top, side = i * virtuals + a * TILE, i * virtuals + b * TILE
                    here = ints[which, top:top + TILE, b * TILE:(b + 1) * TILE]
                    swapped = ints[which, side:side + TILE, a * TILE:(a + 1) * TILE].T
                    gap = base[a * TILE:(a + 1) * TILE, b * TILE:(b + 1) * TILE] - energy - other_energy
                    amps[top:top + TILE, b * TILE:(b + 1) * TILE] = (
                        (2.0 * here - swapped) / gap).astype(jnp.bfloat16)

    def pair_term(block, term, n):
        span = 512

        @pl.loop(0, width // TILE)
        def _(r):
            at = pl.ds(pl.multiple_of(r * TILE, TILE), TILE)
            for c in range(panel // span):
                cols = slice(c * span, (c + 1) * span)
                value = jnp.dot(
                    amps[at, :], block[n * virtuals:(n + 1) * virtuals, cols],
                    preferred_element_type=jnp.float32)
                if n == 0:
                    term[at, cols] = value
                else:
                    term[at, cols] += value

    per_piece = TILE // chunk

    def work(block, which, other, term, piece):
        pair_ints(block, which, piece)
        if piece % 2 == 1:
            pair_amps(which, other, piece // 2)
            pair_term(block, term, piece // 2)

    for c in range(CHUNKS):
        direct[c].wait_recv()
        passed[c].start()
        if c >= 1:
            passed[c - 1].wait_recv()
            if c % per_piece == 0:
                work(far, 1, far_block, far_term, c // per_piece - 1)
        if (c + 1) % per_piece == 0:
            work(near, 0, near_block, near_term, c // per_piece)
    passed[CHUNKS - 1].wait_recv()
    work(far, 1, far_block, far_term, 3)

    @pl.loop(0, width // 64)
    def _(r):
        at = pl.ds(pl.multiple_of(r * 64, 64), 64)
        one, two = near_term[at, :], far_term[at, :]
        partner = jnp.where(even, one, two).astype(jnp.bfloat16).astype(jnp.float32)
        gamma[at, :] = (jnp.where(even, two, one) + partner).astype(jnp.bfloat16)

    for c in range(CHUNKS):
        direct[c].wait_send()
        passed[c].wait_send()


def pair_call(occ_energy, vir_energy, flat):
    width, panel = flat.shape
    virtuals = vir_energy.shape[0]
    block = pltpu.VMEM((width, panel), jnp.bfloat16)
    term = pltpu.VMEM((width, panel), jnp.float32)
    return pl.pallas_call(
        pair_kernel,
        out_shape=jax.ShapeDtypeStruct((width, panel), jnp.bfloat16),
        in_specs=[
            pl.BlockSpec(memory_space=pltpu.SMEM),
            pl.BlockSpec(memory_space=pltpu.VMEM),
            pl.BlockSpec(memory_space=pl.ANY),
        ],
        out_specs=pl.BlockSpec(memory_space=pltpu.VMEM),
        scratch_shapes=[
            block, block, block,
            pltpu.VMEM((2, width, virtuals), jnp.float32),
            pltpu.VMEM((width, virtuals), jnp.bfloat16),
            term, term,
            pltpu.VMEM((virtuals, virtuals), jnp.float32),
            pltpu.SemaphoreType.DMA,
        ] + [pltpu.SemaphoreType.DMA((CHUNKS,))] * 4,
        compiler_params=pltpu.CompilerParams(
            collective_id=0, has_side_effects=True, vmem_limit_bytes=60 * 2**20),
        name="pairs",
    )(occ_energy, vir_energy.reshape(1, virtuals), flat)


def per_device(occ_energy, vir_energy, factors):
    orbitals, virtuals, panel = factors.shape
    width = orbitals * virtuals
    nblocks = lax.axis_size(("occ", "aux"))
    flat = factors.reshape(width, panel)
    gamma_three = pair_call(occ_energy, vir_energy, flat)
    scale = float(orbitals * nblocks * virtuals) ** (-0.5)
    product = lax.dot_general(
        gamma_three, flat, (((0,), (0,)), ((), ())), preferred_element_type=jnp.float32)
    gamma_two = lax.psum_scatter(product * scale, ("occ", "aux"), scatter_dimension=0, tiled=True)
    return gamma_three.reshape(orbitals, virtuals, panel), gamma_two


def solution(mesh):
    placed = (P(), P(), P(("occ", "aux"), None, None))
    return jax.shard_map(
        per_device,
        mesh=mesh,
        in_specs=placed,
        out_specs=(P(("occ", "aux"), None, None), P(("occ", "aux"), None)),
        check_vma=False,
    )
```

```python
import jax
import jax.numpy as jnp
from jax import lax
from jax.experimental import pallas as pl
from jax.experimental.pallas import tpu as pltpu
from jax.sharding import PartitionSpec as P

MESH = pl.DeviceIdType.MESH
NT = (((1,), (1,)), ((), ()))
CHUNKS = 16
TILE = 256


def device(position):
    return (position // 2, position % 2)


def pair_kernel(
    occ, vir, factors, gamma, own, near, far, ints, amps, near_term, far_term, base,
    load_sem, near_send, near_recv, far_send, far_recv,
):
    width, panel = own.shape
    virtuals = vir.shape[1]
    chunk = width // CHUNKS
    count = 2 * lax.axis_size("occ")
    me = lax.axis_index("occ") * 2 + lax.axis_index("aux")
    even = me % 2 == 0
    step = 1 - 2 * (me % 2)
    near_block = (me + step + count) % count
    far_block = (me - step + count) % count
    onward = (me + 2 * step + count) % count
    behind = (me - 2 * step + count) % count

    load = pltpu.make_async_copy(factors, own, load_sem)
    load.start()

    barrier = pltpu.get_barrier_semaphore()
    for other in (near_block, onward, behind):
        pl.semaphore_signal(barrier, inc=1, device_id=device(other), device_id_type=MESH)
    pl.semaphore_wait(barrier, 3)

    def rows(c):
        return pl.ds(c * chunk, chunk)

    direct = [
        pltpu.make_async_remote_copy(
            src_ref=factors.at[rows(c)], dst_ref=near.at[rows(c)],
            send_sem=near_send.at[c], recv_sem=near_recv.at[c],
            device_id=device(near_block), device_id_type=MESH)
        for c in range(CHUNKS)
    ]
    passed = [
        pltpu.make_async_remote_copy(
            src_ref=near.at[rows(c)], dst_ref=far.at[rows(c)],
            send_sem=far_send.at[c], recv_sem=far_recv.at[c],
            device_id=device(onward), device_id_type=MESH)
        for c in range(CHUNKS)
    ]
    for copy in direct:
        copy.start()

    row = jnp.broadcast_to(vir[...], (virtuals, virtuals))
    base[...] = row + row.T
    load.wait()

    def pair_ints(block, which, piece):
        half = piece % 2

        @pl.loop(0, width // TILE)
        def _(r):
            at = pl.ds(pl.multiple_of(r * TILE, TILE), TILE)
            ints[which, at, half * TILE:(half + 1) * TILE] = lax.dot_general(
                own[at, :], block[piece * TILE:(piece + 1) * TILE, :], NT,
                preferred_element_type=jnp.float32)

    def pair_amps(which, other, n):
        other_energy = occ[2 * other + n]
        for i in range(2):
            energy = occ[2 * me + i]
            for a in range(virtuals // TILE):
                for b in range(virtuals // TILE):
                    top, side = i * virtuals + a * TILE, i * virtuals + b * TILE
                    here = ints[which, top:top + TILE, b * TILE:(b + 1) * TILE]
                    swapped = ints[which, side:side + TILE, a * TILE:(a + 1) * TILE].T
                    gap = base[a * TILE:(a + 1) * TILE, b * TILE:(b + 1) * TILE] - energy - other_energy
                    amps[top:top + TILE, b * TILE:(b + 1) * TILE] = (
                        (2.0 * here - swapped) / gap).astype(jnp.bfloat16)

    def pair_term(block, term, n):
        span = 512

        @pl.loop(0, width // TILE)
        def _(r):
            at = pl.ds(pl.multiple_of(r * TILE, TILE), TILE)
            for c in range(panel // span):
                cols = slice(c * span, (c + 1) * span)
                value = jnp.dot(
                    amps[at, :], block[n * virtuals:(n + 1) * virtuals, cols],
                    preferred_element_type=jnp.float32)
                if n == 0:
                    term[at, cols] = value
                else:
                    term[at, cols] += value

    per_piece = TILE // chunk

    def work(block, which, other, term, piece):
        pair_ints(block, which, piece)
        if piece % 2 == 1:
            pair_amps(which, other, piece // 2)
            pair_term(block, term, piece // 2)

    for c in range(CHUNKS):
        direct[c].wait_recv()
        passed[c].start()
        if c >= 1:
            passed[c - 1].wait_recv()
            if c % per_piece == 0:
                work(far, 1, far_block, far_term, c // per_piece - 1)
        if (c + 1) % per_piece == 0:
            work(near, 0, near_block, near_term, c // per_piece)
    passed[CHUNKS - 1].wait_recv()
    work(far, 1, far_block, far_term, 3)

    @pl.loop(0, width // 64)
    def _(r):
        at = pl.ds(pl.multiple_of(r * 64, 64), 64)
        one, two = near_term[at, :], far_term[at, :]
        partner = jnp.where(even, one, two).astype(jnp.bfloat16).astype(jnp.float32)
        gamma[at, :] = (jnp.where(even, two, one) + partner).astype(jnp.bfloat16)

    for c in range(CHUNKS):
        direct[c].wait_send()
        passed[c].wait_send()


def pair_call(occ_energy, vir_energy, flat):
    width, panel = flat.shape
    virtuals = vir_energy.shape[0]
    block = pltpu.VMEM((width, panel), jnp.bfloat16)
    term = pltpu.VMEM((width, panel), jnp.float32)
    return pl.pallas_call(
        pair_kernel,
        out_shape=jax.ShapeDtypeStruct((width, panel), jnp.bfloat16),
        in_specs=[
            pl.BlockSpec(memory_space=pltpu.SMEM),
            pl.BlockSpec(memory_space=pltpu.VMEM),
            pl.BlockSpec(memory_space=pl.ANY),
        ],
        out_specs=pl.BlockSpec(memory_space=pltpu.VMEM),
        scratch_shapes=[
            block, block, block,
            pltpu.VMEM((2, width, virtuals), jnp.float32),
            pltpu.VMEM((width, virtuals), jnp.bfloat16),
            term, term,
            pltpu.VMEM((virtuals, virtuals), jnp.float32),
            pltpu.SemaphoreType.DMA,
        ] + [pltpu.SemaphoreType.DMA((CHUNKS,))] * 4,
        compiler_params=pltpu.CompilerParams(
            collective_id=0, has_side_effects=True, vmem_limit_bytes=60 * 2**20),
        name="pairs",
    )(occ_energy, vir_energy.reshape(1, virtuals), flat)


TN = (((0,), (0,)), ((), ()))
COLS = ((0, 384), (384, 384), (768, 256))
NEAR_FIRST = (2, 1, 3, 0)


def coordinates():
    occ, aux = lax.axis_index("occ"), lax.axis_index("aux")
    return (occ // 8) % 4, (occ // 2) % 4, aux * 2 + occ // 32, occ % 2


def chip(x, y, z, core):
    return ((z % 2) * 32 + x * 8 + y * 2 + core, z // 2)


def sum_kernel(
    gamma_hbm, factors, out, gamma, own, outgoing, incoming, held, part,
    first0, first1, first2, mid0, mid1, mid2, second0, second1, second2,
    late0, late1, late2, third0, third1, third2, rows, rows_in,
    load_sem, core_send, core_recv, send1, recv1, send2, recv2, send3, recv3, end_send, end_recv,
):
    x, y, z, core = coordinates()
    z_lo, z_hi = z % 2, z // 2
    half = out.shape[1] // 2
    mine = pl.multiple_of(core * half, half)
    others = pl.multiple_of((1 - core) * half, half)
    scale = float(128 * gamma.shape[0]) ** (-0.5)

    def along(axis, by):
        place = [x, y, z]
        place[axis] = (place[axis] + by) % 4
        return chip(*place, core)

    load_a = pltpu.make_async_copy(gamma_hbm, gamma, load_sem.at[0])
    load_b = pltpu.make_async_copy(factors, own, load_sem.at[1])
    load_a.start()
    load_b.start()
    barrier = pltpu.get_barrier_semaphore()
    for axis in range(3):
        for by in (1, 2, 3):
            pl.semaphore_signal(barrier, inc=1, device_id=along(axis, by), device_id_type=MESH)
    pl.semaphore_signal(barrier, inc=1, device_id=chip(x, y, z, 1 - core), device_id_type=MESH)
    pl.semaphore_wait(barrier, 10)
    load_a.wait()
    load_b.wait()

    def remote(src, dst, send, recv, target):
        return pltpu.make_async_remote_copy(
            src_ref=src, dst_ref=dst, send_sem=send, recv_sem=recv,
            device_id=target, device_id_type=MESH)

    tiles = [(e, d) for d in NEAR_FIRST for e in (1, 0)]
    swaps = []
    waits = [[], [], []]

    def finish(t):
        e, d = tiles[t]
        zl, xt = (z_lo + e) % 2, (x + d) % 4
        swaps[t].wait_recv()
        for yy in range(4):
            for c in range(2):
                for zh in range(2):
                    at = ((yy * 2 + c) * 2 + zh) * 16
                    total = held[t % 2, at:at + 16, :] + incoming[t, at:at + 16, :].astype(jnp.float32)
                    part[zl, xt, yy, zh, c * 16:(c + 1) * 16, :] = total.astype(jnp.bfloat16)
        copies = []
        if d:
            cols = pl.ds(*COLS[0])
            copies.append((0, part.at[zl, xt, :, :, :, cols], first0.at[d - 1, zl], along(0, d)))
        for by in (2, 1, 3):
            cols = pl.ds(*COLS[1])
            copies.append((1, part.at[zl, xt, (y + by) % 4, :, :, cols], first1.at[by - 1, zl, xt], along(1, by)))
        for by in ((1, 3) if e else (2,)):
            cols = pl.ds(*COLS[2])
            copies.append((2, part.at[zl, xt, :, ((z + by) % 4) // 2, :, cols], first2.at[by - 1, xt], along(2, by)))
        for k, src, dst, target in copies:
            n = sum(len(w) for w in waits)
            copy = remote(src, dst, send1.at[n], recv1.at[n], target)
            copy.start()
            waits[k].append(copy)

    for t, (e, d) in enumerate(tiles):
        zl, xt = (z_lo + e) % 2, (x + d) % 4
        at = pl.ds(pl.multiple_of((zl * 4 + xt) * 256, 256), 256)
        left = gamma[:, at]
        for c in range(2):
            cols = pl.ds(pl.multiple_of(others + c * 512, 512), 512)
            outgoing[t, :, c * 512:(c + 1) * 512] = (lax.dot_general(
                left, own[:, cols], TN, preferred_element_type=jnp.float32) * scale).astype(jnp.bfloat16)
        swap = remote(outgoing.at[t], incoming.at[t], core_send.at[t], core_recv.at[t], chip(x, y, z, 1 - core))
        swap.start()
        swaps.append(swap)
        for c in range(2):
            cols = pl.ds(pl.multiple_of(mine + c * 512, 512), 512)
            held[t % 2, :, c * 512:(c + 1) * 512] = lax.dot_general(
                left, own[:, cols], TN, preferred_element_type=jnp.float32) * scale
        if t:
            finish(t - 1)
    finish(len(tiles) - 1)

    def wide(value):
        return value.astype(jnp.float32)

    seconds = [[], [], []]

    def second(k, by, src, dst, axis):
        n = k * 3 + by - 1
        copy = remote(src, dst, send2.at[n], recv2.at[n], along(axis, by))
        copy.start()
        seconds[k].append(copy)

    for copy in waits[2]:
        copy.wait_recv()
    for xx in range(4):
        for yy in range(4):
            total = wide(part[z_lo, xx, yy, z_hi, :, 768:1024])
            for j in range(3):
                total += wide(first2[j, xx, yy])
            mid2[xx, yy] = total.astype(mid2.dtype)
    for by in (2, 1, 3):
        second(2, by, mid2.at[(x + by) % 4], second2.at[by - 1], 0)

    for copy in waits[0]:
        copy.wait_recv()
    for zl in range(2):
        for yy in range(4):
            for zh in range(2):
                total = wide(part[zl, x, yy, zh, :, 0:384])
                for j in range(3):
                    total += wide(first0[j, zl, yy, zh])
                mid0[yy, zl, zh] = total.astype(mid0.dtype)
    for by in (2, 1, 3):
        second(0, by, mid0.at[(y + by) % 4], second0.at[by - 1], 1)

    for copy in waits[1]:
        copy.wait_recv()
    for zl in range(2):
        for xx in range(4):
            for zh in range(2):
                total = wide(part[zl, xx, y, zh, :, 384:768])
                for j in range(3):
                    total += wide(first1[j, zl, xx, zh])
                mid1[zl, zh, xx] = total.astype(mid1.dtype)
    for by in (2, 1, 3):
        far = (z + by) % 4
        second(1, by, mid1.at[far % 2, far // 2], second1.at[by - 1], 2)

    thirds = [[], [], []]

    def third(k, by, src, dst, axis):
        n = k * 3 + by - 1
        copy = remote(src, dst, send3.at[n], recv3.at[n], along(axis, by))
        copy.start()
        thirds[k].append(copy)

    for copy in seconds[2]:
        copy.wait_recv()
    for yy in range(4):
        total = wide(mid2[x, yy])
        for j in range(3):
            total += wide(second2[j, yy])
        late2[yy] = total
    for by in (2, 1, 3):
        third(2, by, late2.at[(y + by) % 4], third2.at[by - 1], 1)

    for copy in seconds[0]:
        copy.wait_recv()
    for zl in range(2):
        for zh in range(2):
            total = wide(mid0[y, zl, zh])
            for j in range(3):
                total += wide(second0[j, zl, zh])
            late0[zl, zh] = total
    for by in (2, 1, 3):
        far = (z + by) % 4
        third(0, by, late0.at[far % 2, far // 2], third0.at[by - 1], 2)

    for copy in seconds[1]:
        copy.wait_recv()
    for xx in range(4):
        total = wide(mid1[z_lo, z_hi, xx])
        for j in range(3):
            total += wide(second1[j, xx])
        late1[xx] = total
    for by in (2, 1, 3):
        third(1, by, late1.at[(x + by) % 4], third1.at[by - 1], 0)

    for k in (2, 0, 1):
        for copy in thirds[k]:
            copy.wait_recv()
    rows[:, 0:384] = late0[z_lo, z_hi] + third0[0] + third0[1] + third0[2]
    rows[:, 384:768] = late1[x] + third1[0] + third1[1] + third1[2]
    rows[:, 768:1024] = late2[y] + third2[0] + third2[1] + third2[2]
    last = remote(
        rows.at[pl.ds(pl.multiple_of((1 - core) * 16, 16), 16)], rows_in, end_send, end_recv,
        chip(x, y, z, 1 - core))
    last.start()
    out[:, pl.ds(mine, half)] = rows[pl.ds(pl.multiple_of(core * 16, 16), 16), :]
    last.wait_recv()
    out[:, pl.ds(others, half)] = rows_in[...]

    for copy in swaps + waits[0] + waits[1] + waits[2] + sum(seconds, []) + sum(thirds, []) + [last]:
        copy.wait_send()


def sum_call(gamma, flat):
    width, panel = flat.shape
    half = panel // 2
    low, full = jnp.bfloat16, jnp.float32
    dma = pltpu.SemaphoreType.DMA
    return pl.pallas_call(
        sum_kernel,
        out_shape=jax.ShapeDtypeStruct((16, panel), jnp.float32),
        in_specs=[pl.BlockSpec(memory_space=pl.ANY)] * 2,
        out_specs=pl.BlockSpec(memory_space=pltpu.VMEM),
        scratch_shapes=[
            pltpu.VMEM((width, panel), low),
            pltpu.VMEM((width, panel), low),
            pltpu.VMEM((8, 256, half), low),
            pltpu.VMEM((8, 256, half), low),
            pltpu.VMEM((2, 256, half), full),
            pltpu.VMEM((2, 4, 4, 2, 32, half), low),
            pltpu.VMEM((3, 2, 4, 2, 32, 384), low),
            pltpu.VMEM((3, 2, 4, 2, 32, 384), low),
            pltpu.VMEM((3, 4, 4, 32, 256), low),
            pltpu.VMEM((4, 2, 2, 32, 384), low),
            pltpu.VMEM((2, 2, 4, 32, 384), low),
            pltpu.VMEM((4, 4, 32, 256), low),
            pltpu.VMEM((3, 2, 2, 32, 384), low),
            pltpu.VMEM((3, 4, 32, 384), low),
            pltpu.VMEM((3, 4, 32, 256), low),
            pltpu.VMEM((2, 2, 32, 384), full),
            pltpu.VMEM((4, 32, 384), full),
            pltpu.VMEM((4, 32, 256), full),
            pltpu.VMEM((3, 32, 384), full),
            pltpu.VMEM((3, 32, 384), full),
            pltpu.VMEM((3, 32, 256), full),
            pltpu.VMEM((32, half), full),
            pltpu.VMEM((16, half), full),
            dma((2,)), dma((8,)), dma((8,)), dma((42,)), dma((42,)),
            dma((9,)), dma((9,)), dma((9,)), dma((9,)), dma, dma,
        ],
        compiler_params=pltpu.CompilerParams(
            collective_id=1, has_side_effects=True, vmem_limit_bytes=60 * 2**20),
        name="sums",
    )(gamma, flat)


def per_device(occ_energy, vir_energy, factors):
    orbitals, virtuals, panel = factors.shape
    width = orbitals * virtuals
    flat = factors.reshape(width, panel)
    gamma_three = pair_call(occ_energy, vir_energy, flat)
    gamma_two = sum_call(gamma_three, flat)
    return gamma_three.reshape(orbitals, virtuals, panel), gamma_two


def solution(mesh):
    placed = (P(), P(), P(("occ", "aux"), None, None))
    return jax.shard_map(
        per_device,
        mesh=mesh,
        in_specs=placed,
        out_specs=(P(("occ", "aux"), None, None), P(("occ", "aux"), None)),
        check_vma=False,
    )
```

```python
import jax
import jax.numpy as jnp
from jax import lax
from jax.experimental import pallas as pl
from jax.experimental.pallas import tpu as pltpu
from jax.sharding import PartitionSpec as P

MESH = pl.DeviceIdType.MESH
NT = (((1,), (1,)), ((), ()))
TN = (((0,), (0,)), ((), ()))
CHUNKS = 16
LAG = 3
TILE = 256
COLS = ((0, 384), (384, 384), (768, 256))
NEAR_FIRST = (2, 1, 3, 0)
SLOTS = 4


def device(position):
    return (position // 2, position % 2)


def by_plane(z, values):
    return jnp.where(z == 0, values[0], jnp.where(z == 1, values[1], jnp.where(z == 2, values[2], values[3])))


def coordinates():
    occ, aux = lax.axis_index("occ"), lax.axis_index("aux")
    return (occ // 8) % 4, (occ // 2) % 4, aux * 2 + occ // 32, occ % 2


def chip(x, y, z, core):
    return ((z % 2) * 32 + x * 8 + y * 2 + core, z // 2)


def density_kernel(
    occ, vir, factors, gamma_out, out, own, near, far, ints, amps, near_term, far_term, base, transit,
    gamma, outgoing, incoming, part,
    first0, first1, first2, mid0, mid1, mid2, second0, second1, second2,
    late0, late1, late2, third0, third1, third2, rows, rows_in,
    load_sem, near_send, near_recv, far_send, far_recv, transit_send, transit_recv,
    store_sem, core_send, core_recv, send1, recv1, send2, recv2, send3, recv3, end_send, end_recv,
):
    width, panel = own.shape
    virtuals = vir.shape[1]
    chunk = width // CHUNKS
    count = 2 * lax.axis_size("occ")
    me = lax.axis_index("occ") * 2 + lax.axis_index("aux")
    even = me % 2 == 0
    step = 1 - 2 * (me % 2)
    near_block = (me + step + count) % count
    far_block = (me - step + count) % count
    onward = (me + 2 * step + count) % count
    behind = (me - 2 * step + count) % count

    x, y, z, core = coordinates()
    column = jnp.where(z < 2, x * 4 + y, 15 - (x * 4 + y))
    crosses = me % 64 == jnp.where(even, 62, 1)
    crossed = (me % 64 == 0) | (me % 64 == 63)
    relays = core == jnp.where(z < 2, 1, 0)
    relay_from = by_plane(z, (126, 62, 65, 1))
    relay_to = by_plane(z, (0, 64, 63, 127))

    def relay_of(c, plane):
        at = jnp.where(plane < 2, c * 2 + 1, (CHUNKS - 1 - c) * 2)
        return ((plane % 2) * 32 + at, plane // 2)

    plane_on = by_plane(z, (1, 0, 3, 2))

    z_lo, z_hi = z % 2, z // 2
    half = panel // 2
    mine = pl.multiple_of(core * half, half)
    others = pl.multiple_of((1 - core) * half, half)
    scale = float(count * width) ** (-0.5)

    def along(axis, by):
        place = [x, y, z]
        place[axis] = (place[axis] + by) % 4
        return chip(*place, core)

    def remote(src, dst, send, recv, target):
        return pltpu.make_async_remote_copy(
            src_ref=src, dst_ref=dst, send_sem=send, recv_sem=recv,
            device_id=target, device_id_type=MESH)

    load = pltpu.make_async_copy(factors, own, load_sem)
    load.start()

    barrier = pltpu.get_barrier_semaphore()
    for other in (near_block, onward, behind):
        pl.semaphore_signal(barrier, inc=1, device_id=device(other), device_id_type=MESH)
    for axis in range(3):
        for by in (1, 2, 3):
            pl.semaphore_signal(barrier, inc=1, device_id=along(axis, by), device_id_type=MESH)
    pl.semaphore_signal(barrier, inc=1, device_id=chip(x, y, z, 1 - core), device_id_type=MESH)

    @pl.when(crossed)
    def _():
        for c in range(CHUNKS):
            pl.semaphore_signal(barrier, inc=1, device_id=relay_of(c, z), device_id_type=MESH)

    @pl.when(relays)
    def _():
        pl.semaphore_signal(barrier, inc=1, device_id=device(relay_from), device_id_type=MESH)

    pl.semaphore_wait(barrier, 13 + jnp.where(crosses, CHUNKS, 0) + jnp.where(relays, 1, 0))

    def span(c):
        return pl.ds(c * chunk, chunk)

    direct = [
        pltpu.make_async_remote_copy(
            src_ref=factors.at[span(c)], dst_ref=near.at[span(c)],
            send_sem=near_send.at[c], recv_sem=near_recv.at[c],
            device_id=device(near_block), device_id_type=MESH)
        for c in range(CHUNKS)
    ]
    passed = [
        pltpu.make_async_remote_copy(
            src_ref=near.at[span(c)], dst_ref=far.at[span(c)],
            send_sem=far_send.at[c], recv_sem=far_recv.at[c],
            device_id=device(onward), device_id_type=MESH)
        for c in range(CHUNKS)
    ]
    crossing = [
        pltpu.make_async_remote_copy(
            src_ref=near.at[span(c)], dst_ref=transit,
            send_sem=far_send.at[c], recv_sem=transit_recv,
            device_id=relay_of(c, plane_on), device_id_type=MESH)
        for c in range(CHUNKS)
    ]
    relayed = pltpu.make_async_remote_copy(
        src_ref=transit, dst_ref=far.at[pl.ds(pl.multiple_of(column * chunk, chunk), chunk)],
        send_sem=transit_send, recv_sem=far_recv.at[column],
        device_id=device(relay_to), device_id_type=MESH)
    for copy in direct:
        copy.start()

    def pass_on(c):
        pl.when(crosses)(crossing[c].start)
        pl.when(jnp.logical_not(crosses))(passed[c].start)

    def relay(c):
        @pl.when(relays & (column == c))
        def _():
            crossing[c].wait_recv()
            relayed.start()

    row = jnp.broadcast_to(vir[...], (virtuals, virtuals))
    base[...] = row + row.T
    load.wait()

    def pair_ints(block, which, piece):
        left = piece % 2 * TILE

        @pl.loop(0, width // 512)
        def _(r):
            at = pl.ds(pl.multiple_of(r * 512, 512), 512)
            ints[which, at, left:left + TILE] = lax.dot_general(
                own[at, :], block[piece * TILE:(piece + 1) * TILE, :], NT,
                preferred_element_type=jnp.float32)

    def pair_amps(which, other, n):
        other_energy = occ[2 * other + n]
        for i in range(2):
            energy = occ[2 * me + i]
            for a in range(virtuals // TILE):
                for b in range(virtuals // TILE):
                    top, side = i * virtuals + a * TILE, i * virtuals + b * TILE
                    here = ints[which, top:top + TILE, b * TILE:(b + 1) * TILE]
                    swapped = ints[which, side:side + TILE, a * TILE:(a + 1) * TILE].T
                    gap = base[a * TILE:(a + 1) * TILE, b * TILE:(b + 1) * TILE] - energy - other_energy
                    amps[which, top:top + TILE, b * TILE:(b + 1) * TILE] = (
                        (2.0 * here - swapped) / gap).astype(jnp.bfloat16)

    def pair_term(which, block, term):
        @pl.loop(0, width // TILE)
        def _(r):
            at = pl.ds(pl.multiple_of(r * TILE, TILE), TILE)
            for c in range(0, panel, 512):
                term[at, c:c + 512] = jnp.dot(
                    amps[which, at, :], block[0:virtuals, c:c + 512], preferred_element_type=jnp.float32)

    per_piece = TILE // chunk

    def work(block, which, other, term, piece):
        pair_ints(block, which, piece)
        if piece % 2 == 1:
            pair_amps(which, other, piece // 2)
            if piece == 1:
                pair_term(which, block, term)

    for c in range(CHUNKS):
        direct[c].wait_recv()
        pass_on(c)
        if c >= 2:
            relay(c - 2)
        if c >= LAG:
            passed[c - LAG].wait_recv()
            if (c - LAG + 1) % per_piece == 0:
                work(far, 1, far_block, far_term, (c - LAG) // per_piece)
        if (c + 1) % per_piece == 0:
            work(near, 0, near_block, near_term, c // per_piece)
    relay(CHUNKS - 2)
    relay(CHUNKS - 1)
    for c in range(CHUNKS - LAG, CHUNKS):
        passed[c].wait_recv()
    work(far, 1, far_block, far_term, 3)

    tiles = [(e, d) for d in NEAR_FIRST for e in (1, 0)]
    swaps = []
    waits = [[], [], []]

    def finish(t):
        e, d = tiles[t]
        zl, xt = (z_lo + e) % 2, (x + d) % 4
        swaps[t].wait_recv()
        for yy in range(4):
            for c in range(2):
                for zh in range(2):
                    at = ((yy * 2 + c) * 2 + zh) * 16
                    total = jnp.concatenate(
                        [ints[t % 2, at:at + 16, :], ints[t % 2, TILE + at:TILE + at + 16, :]], axis=1)
                    total += incoming[t, at:at + 16, :].astype(jnp.float32)
                    part[zl, xt, yy, zh, c * 16:(c + 1) * 16, :] = total.astype(jnp.bfloat16)
        copies = []
        if d:
            cols = pl.ds(*COLS[0])
            copies.append((0, part.at[zl, xt, :, :, :, cols], first0.at[d - 1, zl], along(0, d)))
        for by in (2, 1, 3):
            cols = pl.ds(*COLS[1])
            copies.append((1, part.at[zl, xt, (y + by) % 4, :, :, cols], first1.at[by - 1, zl, xt], along(1, by)))
        for by in ((1, 3) if e else (2,)):
            cols = pl.ds(*COLS[2])
            copies.append((2, part.at[zl, xt, :, ((z + by) % 4) // 2, :, cols], first2.at[by - 1, xt], along(2, by)))
        for k, src, dst, target in copies:
            n = sum(len(w) for w in waits)
            copy = remote(src, dst, send1.at[n], recv1.at[n], target)
            copy.start()
            waits[k].append(copy)

    stores = []
    for t, (e, d) in enumerate(tiles):
        zl, xt = (z_lo + e) % 2, (x + d) % 4
        at = pl.ds(pl.multiple_of((zl * 4 + xt) * TILE, TILE), TILE)

        @pl.loop(0, width // 512)
        def _(r):
            group = pl.ds(pl.multiple_of(r * 512, 512), 512)
            one = near_term[group, at] + jnp.dot(
                amps[0, group, :], near[virtuals:width, at], preferred_element_type=jnp.float32)
            two = far_term[group, at] + jnp.dot(
                amps[1, group, :], far[virtuals:width, at], preferred_element_type=jnp.float32)
            partner = jnp.where(even, one, two).astype(jnp.bfloat16).astype(jnp.float32)
            gamma[group, at] = (jnp.where(even, two, one) + partner).astype(jnp.bfloat16)

        store = pltpu.make_async_copy(gamma.at[:, at], gamma_out.at[:, at], store_sem.at[t])
        store.start()
        stores.append(store)
        left = gamma[:, at]
        if t >= SLOTS:
            swaps[t - SLOTS].wait_send()
        for c in range(0, half, 512):
            cols = pl.ds(pl.multiple_of(others + c, 512), 512)
            outgoing[t % SLOTS, :, c:c + 512] = (lax.dot_general(
                left, own[:, cols], TN, preferred_element_type=jnp.float32) * scale).astype(jnp.bfloat16)
        swap = remote(
            outgoing.at[t % SLOTS], incoming.at[t], core_send.at[t], core_recv.at[t], chip(x, y, z, 1 - core))
        swap.start()
        swaps.append(swap)
        for c in range(2):
            cols = pl.ds(pl.multiple_of(mine + c * 512, 512), 512)
            ints[t % 2, c * TILE:(c + 1) * TILE, :] = lax.dot_general(
                left, own[:, cols], TN, preferred_element_type=jnp.float32) * scale
        if t:
            finish(t - 1)
    finish(len(tiles) - 1)

    def wide(value):
        return value.astype(jnp.float32)

    seconds = [[], [], []]

    def second(k, by, src, dst, axis):
        n = k * 3 + by - 1
        copy = remote(src, dst, send2.at[n], recv2.at[n], along(axis, by))
        copy.start()
        seconds[k].append(copy)

    for copy in waits[2]:
        copy.wait_recv()
    for xx in range(4):
        for yy in range(4):
            total = wide(part[z_lo, xx, yy, z_hi, :, 768:1024])
            for j in range(3):
                total += wide(first2[j, xx, yy])
            mid2[xx, yy] = total.astype(mid2.dtype)
    for by in (2, 1, 3):
        second(2, by, mid2.at[(x + by) % 4], second2.at[by - 1], 0)

    for copy in waits[0]:
        copy.wait_recv()
    for zl in range(2):
        for yy in range(4):
            for zh in range(2):
                total = wide(part[zl, x, yy, zh, :, 0:384])
                for j in range(3):
                    total += wide(first0[j, zl, yy, zh])
                mid0[yy, zl, zh] = total.astype(mid0.dtype)
    for by in (2, 1, 3):
        second(0, by, mid0.at[(y + by) % 4], second0.at[by - 1], 1)

    for copy in waits[1]:
        copy.wait_recv()
    for zl in range(2):
        for xx in range(4):
            for zh in range(2):
                total = wide(part[zl, xx, y, zh, :, 384:768])
                for j in range(3):
                    total += wide(first1[j, zl, xx, zh])
                mid1[zl, zh, xx] = total.astype(mid1.dtype)
    for by in (2, 1, 3):
        far = (z + by) % 4
        second(1, by, mid1.at[far % 2, far // 2], second1.at[by - 1], 2)

    thirds = [[], [], []]

    def third(k, by, src, dst, axis):
        n = k * 3 + by - 1
        copy = remote(src, dst, send3.at[n], recv3.at[n], along(axis, by))
        copy.start()
        thirds[k].append(copy)

    for copy in seconds[2]:
        copy.wait_recv()
    for yy in range(4):
        total = wide(mid2[x, yy])
        for j in range(3):
            total += wide(second2[j, yy])
        late2[yy] = total
    for by in (2, 1, 3):
        third(2, by, late2.at[(y + by) % 4], third2.at[by - 1], 1)

    for copy in seconds[0]:
        copy.wait_recv()
    for zl in range(2):
        for zh in range(2):
            total = wide(mid0[y, zl, zh])
            for j in range(3):
                total += wide(second0[j, zl, zh])
            late0[zl, zh] = total
    for by in (2, 1, 3):
        far = (z + by) % 4
        third(0, by, late0.at[far % 2, far // 2], third0.at[by - 1], 2)

    for copy in seconds[1]:
        copy.wait_recv()
    for xx in range(4):
        total = wide(mid1[z_lo, z_hi, xx])
        for j in range(3):
            total += wide(second1[j, xx])
        late1[xx] = total
    for by in (2, 1, 3):
        third(1, by, late1.at[(x + by) % 4], third1.at[by - 1], 0)

    for k in (2, 0, 1):
        for copy in thirds[k]:
            copy.wait_recv()
    rows[:, 0:384] = late0[z_lo, z_hi] + third0[0] + third0[1] + third0[2]
    rows[:, 384:768] = late1[x] + third1[0] + third1[1] + third1[2]
    rows[:, 768:1024] = late2[y] + third2[0] + third2[1] + third2[2]
    last = remote(
        rows.at[pl.ds(pl.multiple_of((1 - core) * 16, 16), 16)], rows_in, end_send, end_recv,
        chip(x, y, z, 1 - core))
    last.start()
    out[:, pl.ds(mine, half)] = rows[pl.ds(pl.multiple_of(core * 16, 16), 16), :]
    last.wait_recv()
    out[:, pl.ds(others, half)] = rows_in[...]

    for c in range(CHUNKS):
        direct[c].wait_send()
        passed[c].wait_send()
    pl.when(relays)(relayed.wait_send)
    for store in stores:
        store.wait()
    for copy in swaps[-SLOTS:] + waits[0] + waits[1] + waits[2] + sum(seconds, []) + sum(thirds, []) + [last]:
        copy.wait_send()


def density_call(occ_energy, vir_energy, flat):
    width, panel = flat.shape
    virtuals = vir_energy.shape[0]
    half = panel // 2
    low, full = jnp.bfloat16, jnp.float32
    dma = pltpu.SemaphoreType.DMA
    block = pltpu.VMEM((width, panel), low)
    term = pltpu.VMEM((width, panel), full)
    return pl.pallas_call(
        density_kernel,
        out_shape=(
            jax.ShapeDtypeStruct((width, panel), low),
            jax.ShapeDtypeStruct((16, panel), full),
        ),
        in_specs=[
            pl.BlockSpec(memory_space=pltpu.SMEM),
            pl.BlockSpec(memory_space=pltpu.VMEM),
            pl.BlockSpec(memory_space=pl.ANY),
        ],
        out_specs=(pl.BlockSpec(memory_space=pl.ANY), pl.BlockSpec(memory_space=pltpu.VMEM)),
        scratch_shapes=[
            block, block, block,
            pltpu.VMEM((2, width, virtuals), full),
            pltpu.VMEM((2, width, virtuals), low),
            term, term,
            pltpu.VMEM((virtuals, virtuals), full),
            pltpu.VMEM((width // CHUNKS, panel), low),
            block,
            pltpu.VMEM((SLOTS, TILE, half), low),
            pltpu.VMEM((8, TILE, half), low),
            pltpu.VMEM((2, 4, 4, 2, 32, half), low),
            pltpu.VMEM((3, 2, 4, 2, 32, 384), low),
            pltpu.VMEM((3, 2, 4, 2, 32, 384), low),
            pltpu.VMEM((3, 4, 4, 32, 256), low),
            pltpu.VMEM((4, 2, 2, 32, 384), low),
            pltpu.VMEM((2, 2, 4, 32, 384), low),
            pltpu.VMEM((4, 4, 32, 256), low),
            pltpu.VMEM((3, 2, 2, 32, 384), low),
            pltpu.VMEM((3, 4, 32, 384), low),
            pltpu.VMEM((3, 4, 32, 256), low),
            pltpu.VMEM((2, 2, 32, 384), full),
            pltpu.VMEM((4, 32, 384), full),
            pltpu.VMEM((4, 32, 256), full),
            pltpu.VMEM((3, 32, 384), full),
            pltpu.VMEM((3, 32, 384), full),
            pltpu.VMEM((3, 32, 256), full),
            pltpu.VMEM((32, half), full),
            pltpu.VMEM((16, half), full),
            dma, dma((CHUNKS,)), dma((CHUNKS,)), dma((CHUNKS,)), dma((CHUNKS,)), dma, dma,
            dma((8,)), dma((8,)), dma((8,)), dma((42,)), dma((42,)),
            dma((9,)), dma((9,)), dma((9,)), dma((9,)), dma, dma,
        ],
        compiler_params=pltpu.CompilerParams(
            collective_id=0, has_side_effects=True, vmem_limit_bytes=62 * 2**20),
        name="densities",
    )(occ_energy, vir_energy.reshape(1, virtuals), flat)


def per_device(occ_energy, vir_energy, factors):
    orbitals, virtuals, panel = factors.shape
    flat = factors.reshape(orbitals * virtuals, panel)
    gamma_three, gamma_two = density_call(occ_energy, vir_energy, flat)
    return gamma_three.reshape(orbitals, virtuals, panel), gamma_two


def solution(mesh):
    placed = (P(), P(), P(("occ", "aux"), None, None))
    return jax.shard_map(
        per_device,
        mesh=mesh,
        in_specs=placed,
        out_specs=(P(("occ", "aux"), None, None), P(("occ", "aux"), None)),
        check_vma=False,
    )
```

```python
import jax
import jax.numpy as jnp
from jax import lax
from jax.experimental import pallas as pl
from jax.experimental.pallas import tpu as pltpu
from jax.sharding import PartitionSpec as P

MESH = pl.DeviceIdType.MESH
NT = (((1,), (1,)), ((), ()))
TN = (((0,), (0,)), ((), ()))
SIZES = (64,) * 14 + (32, 32, 32, 16, 16)
STARTS = tuple(sum(SIZES[:c]) for c in range(len(SIZES)))
CHUNKS = len(SIZES)
RELAYS = 16
LAG = 3
TILE = 256
COLS = ((0, 384), (384, 384), (768, 256))
NEAR_FIRST = (2, 1, 3, 0)


def device(position):
    return (position // 2, position % 2)


def by_plane(z, values):
    return jnp.where(z == 0, values[0], jnp.where(z == 1, values[1], jnp.where(z == 2, values[2], values[3])))


def coordinates():
    occ, aux = lax.axis_index("occ"), lax.axis_index("aux")
    return (occ // 8) % 4, (occ // 2) % 4, aux * 2 + occ // 32, occ % 2


def chip(x, y, z, core):
    return ((z % 2) * 32 + x * 8 + y * 2 + core, z // 2)


def density_kernel(
    occ, vir, factors, gamma_out, out, own, near, far, ints, amps, term, base, transit,
    gamma, turned, other_turned, other_own, part,
    first0, first1, first2, mid0, mid1, mid2, second0, second1, second2,
    late0, late1, late2, third0, third1, third2, rows, rows_in,
    load_sem, near_send, near_recv, far_send, far_recv, cross_send, cross_recv,
    transit_send, transit_recv, half_send, half_recv,
    store_sem, core_send, core_recv, send1, recv1, send2, recv2, send3, recv3, end_send, end_recv,
):
    width, panel = own.shape
    virtuals = vir.shape[1]
    strip = width // RELAYS
    count = 2 * lax.axis_size("occ")
    me = lax.axis_index("occ") * 2 + lax.axis_index("aux")
    even = me % 2 == 0
    step = 1 - 2 * (me % 2)
    near_block = (me + step + count) % count
    far_block = (me - step + count) % count
    onward = (me + 2 * step + count) % count
    behind = (me - 2 * step + count) % count

    x, y, z, core = coordinates()
    column = jnp.where(z < 2, x * 4 + y, 15 - (x * 4 + y))
    ends = me % 64 == jnp.where(even, 62, 1)
    crosses = (me % 64 == 0) | (me % 64 == 63)
    direct_far = jnp.logical_not(crosses)
    relays = core == jnp.where(z < 2, 1, 0)
    relay_from = by_plane(z, (127, 63, 64, 0))
    relay_to = by_plane(z, (0, 64, 63, 127))

    def relay_of(c, plane):
        at = jnp.where(plane < 2, c * 2 + 1, (RELAYS - 1 - c) * 2)
        return ((plane % 2) * 32 + at, plane // 2)

    plane_on = by_plane(z, (3, 2, 1, 0))

    z_lo, z_hi = z % 2, z // 2
    half = panel // 2
    mine = pl.multiple_of(core * half, half)
    others = pl.multiple_of((1 - core) * half, half)
    scale = float(count * width) ** (-0.5)

    def along(axis, by):
        place = [x, y, z]
        place[axis] = (place[axis] + by) % 4
        return chip(*place, core)

    def remote(src, dst, send, recv, target):
        return pltpu.make_async_remote_copy(
            src_ref=src, dst_ref=dst, send_sem=send, recv_sem=recv,
            device_id=target, device_id_type=MESH)

    load = pltpu.make_async_copy(factors, own, load_sem)
    load.start()

    barrier = pltpu.get_barrier_semaphore()
    for other in (near_block, onward, behind):
        pl.semaphore_signal(barrier, inc=1, device_id=device(other), device_id_type=MESH)
    for axis in range(3):
        for by in (1, 2, 3):
            pl.semaphore_signal(barrier, inc=1, device_id=along(axis, by), device_id_type=MESH)
    pl.semaphore_signal(barrier, inc=1, device_id=chip(x, y, z, 1 - core), device_id_type=MESH)

    @pl.when(crosses)
    def _():
        for c in range(RELAYS):
            pl.semaphore_signal(barrier, inc=1, device_id=relay_of(c, z), device_id_type=MESH)

    @pl.when(relays)
    def _():
        pl.semaphore_signal(barrier, inc=1, device_id=device(relay_from), device_id_type=MESH)

    pl.semaphore_wait(barrier, 13 + jnp.where(crosses, RELAYS, 0) + jnp.where(relays, 1, 0))

    def span(c):
        return pl.ds(STARTS[c], SIZES[c])

    def strip_at(k):
        return pl.ds(k * strip, strip)

    direct = [
        pltpu.make_async_remote_copy(
            src_ref=factors.at[span(c)], dst_ref=near.at[span(c)],
            send_sem=near_send.at[c], recv_sem=near_recv.at[c],
            device_id=device(near_block), device_id_type=MESH)
        for c in range(CHUNKS)
    ]
    passed = [
        pltpu.make_async_remote_copy(
            src_ref=near.at[span(c)], dst_ref=far.at[span(c)],
            send_sem=far_send.at[c], recv_sem=far_recv.at[c],
            device_id=device(onward), device_id_type=MESH)
        for c in range(CHUNKS)
    ]
    crossing = [
        pltpu.make_async_remote_copy(
            src_ref=factors.at[strip_at(k)], dst_ref=transit,
            send_sem=cross_send.at[k], recv_sem=transit_recv,
            device_id=relay_of(k, plane_on), device_id_type=MESH)
        for k in range(RELAYS)
    ]
    landing = [
        pltpu.make_async_remote_copy(
            src_ref=transit, dst_ref=far.at[strip_at(k)],
            send_sem=transit_send, recv_sem=cross_recv.at[k],
            device_id=device(relay_to), device_id_type=MESH)
        for k in range(RELAYS)
    ]
    relayed = pltpu.make_async_remote_copy(
        src_ref=transit, dst_ref=far.at[pl.ds(pl.multiple_of(column * strip, strip), strip)],
        send_sem=transit_send, recv_sem=cross_recv.at[column],
        device_id=device(relay_to), device_id_type=MESH)
    for copy in direct:
        copy.start()
    half_swap = remote(factors.at[:, pl.ds(others, half)], other_own, half_send, half_recv, chip(x, y, z, 1 - core))
    half_swap.start()

    def relay(k):
        @pl.when(relays & (column == k))
        def _():
            crossing[k].wait_recv()
            relayed.start()

    row = jnp.broadcast_to(vir[...], (virtuals, virtuals))
    base[...] = row + row.T
    load.wait()

    def pair_ints(block, which, piece):
        left = piece % 2 * TILE

        @pl.loop(0, width // 512)
        def _(r):
            at = pl.ds(pl.multiple_of(r * 512, 512), 512)
            ints[which, at, left:left + TILE] = lax.dot_general(
                own[at, :], block[piece * TILE:(piece + 1) * TILE, :], NT,
                preferred_element_type=jnp.float32)

    def pair_amps(which, other, n):
        other_energy = occ[2 * other + n]
        for i in range(2):
            energy = occ[2 * me + i]
            for a in range(virtuals // TILE):
                for b in range(virtuals // TILE):
                    top, side = i * virtuals + a * TILE, i * virtuals + b * TILE
                    here = ints[which, top:top + TILE, b * TILE:(b + 1) * TILE]
                    swapped = ints[which, side:side + TILE, a * TILE:(a + 1) * TILE].T
                    gap = base[a * TILE:(a + 1) * TILE, b * TILE:(b + 1) * TILE] - energy - other_energy
                    amps[which, top:top + TILE, b * TILE:(b + 1) * TILE] = (
                        (2.0 * here - swapped) / gap).astype(jnp.bfloat16)

    def pair_term(which, block, n, first=False):
        @pl.loop(0, width // 512)
        def _(r):
            at = pl.ds(pl.multiple_of(r * 512, 512), 512)
            for c in range(0, panel, 512):
                value = jnp.dot(
                    amps[which, at, :], block[n * virtuals:(n + 1) * virtuals, c:c + 512],
                    preferred_element_type=jnp.float32)
                if not first:
                    value += term[at, c:c + 512]
                term[at, c:c + 512] = value

    def far_piece(piece):
        @pl.when(crosses)
        def _():
            for k in range(piece * 4, piece * 4 + 4):
                landing[k].wait_recv()

        pair_ints(far, 1, piece)
        if piece % 2 == 1:
            pair_amps(1, far_block, piece // 2)
        if piece == 1:
            pair_term(1, far, 0)

    def near_piece(piece):
        pair_ints(near, 0, piece)
        if piece % 2 == 1:
            pair_amps(0, near_block, piece // 2)
            pair_term(0, near, piece // 2, first=piece == 1)

    ends_of = {STARTS[c] + SIZES[c]: c for c in range(CHUNKS)}
    whole = {ends_of[(p + 1) * TILE]: p for p in range(width // TILE)}
    for c in range(CHUNKS):
        direct[c].wait_recv()
        pl.when(jnp.logical_not(ends))(passed[c].start)
        if 2 * c < RELAYS:
            pl.when(crosses)(crossing[2 * c].start)
            pl.when(crosses)(crossing[2 * c + 1].start)
        if 0 <= 2 * (c - 3) < RELAYS:
            relay(2 * (c - 3))
            relay(2 * (c - 3) + 1)
        if c >= LAG:
            pl.when(direct_far)(passed[c - LAG].wait_recv)
            if c - LAG in whole:
                far_piece(whole[c - LAG])
        if c in whole:
            near_piece(whole[c])
    for c in range(CHUNKS - LAG, CHUNKS):
        pl.when(direct_far)(passed[c].wait_recv)
    far_piece(3)

    tiles = [(e, d) for d in NEAR_FIRST for e in (1, 0)]
    swaps = []
    stores = []
    waits = [[], [], []]

    def columns(t):
        e, d = tiles[t]
        zl, xt = (z_lo + e) % 2, (x + d) % 4
        return zl, xt, pl.ds(pl.multiple_of((zl * 4 + xt) * TILE, TILE), TILE)

    def tile_term(t):
        _, _, at = columns(t)
        for r in range(0, width, 512):
            value = term[r:r + 512, at] + jnp.dot(
                amps[1, r:r + 512, :], far[virtuals:width, at], preferred_element_type=jnp.float32)
            value = value.astype(jnp.bfloat16)
            gamma[r:r + 512, at] = value
            turned[t, :, r:r + 512] = value.T
        store = pltpu.make_async_copy(gamma.at[:, at], gamma_out.at[:, at], store_sem.at[t])
        store.start()
        stores.append(store)
        swap = remote(turned.at[t], other_turned.at[t], core_send.at[t], core_recv.at[t], chip(x, y, z, 1 - core))
        swap.start()
        swaps.append(swap)

    def finish(t):
        e, d = tiles[t]
        zl, xt, _ = columns(t)
        swaps[t].wait_recv()
        for c in range(0, half, 512):
            total = jnp.dot(
                turned[t], own[:, pl.ds(pl.multiple_of(mine + c, 512), 512)], preferred_element_type=jnp.float32)
            total += jnp.dot(other_turned[t], other_own[:, c:c + 512], preferred_element_type=jnp.float32)
            total = (total * scale).astype(jnp.bfloat16)
            for yy in range(4):
                for cc in range(2):
                    for zh in range(2):
                        at = ((yy * 2 + cc) * 2 + zh) * 16
                        part[zl, xt, yy, zh, cc * 16:(cc + 1) * 16, c:c + 512] = total[at:at + 16, :]
        copies = []
        if d:
            cols = pl.ds(*COLS[0])
            copies.append((0, part.at[zl, xt, :, :, :, cols], first0.at[d - 1, zl], along(0, d)))
        for by in (2, 1, 3):
            cols = pl.ds(*COLS[1])
            copies.append((1, part.at[zl, xt, (y + by) % 4, :, :, cols], first1.at[by - 1, zl, xt], along(1, by)))
        for by in ((1, 3) if e else (2,)):
            cols = pl.ds(*COLS[2])
            copies.append((2, part.at[zl, xt, :, ((z + by) % 4) // 2, :, cols], first2.at[by - 1, xt], along(2, by)))
        for k, src, dst, target in copies:
            n = sum(len(w) for w in waits)
            copy = remote(src, dst, send1.at[n], recv1.at[n], target)
            copy.start()
            waits[k].append(copy)

    half_swap.wait_recv()
    for t in range(len(tiles)):
        tile_term(t)
        if t:
            finish(t - 1)
    finish(len(tiles) - 1)

    def wide(value):
        return value.astype(jnp.float32)

    seconds = [[], [], []]

    def second(k, by, src, dst, axis):
        n = k * 3 + by - 1
        copy = remote(src, dst, send2.at[n], recv2.at[n], along(axis, by))
        copy.start()
        seconds[k].append(copy)

    for copy in waits[0]:
        copy.wait_recv()
    for zl in range(2):
        for yy in range(4):
            for zh in range(2):
                total = wide(part[zl, x, yy, zh, :, 0:384])
                for j in range(3):
                    total += wide(first0[j, zl, yy, zh])
                mid0[yy, zl, zh] = total.astype(mid0.dtype)
    for by in (2, 1, 3):
        second(0, by, mid0.at[(y + by) % 4], second0.at[by - 1], 1)

    for copy in waits[1]:
        copy.wait_recv()
    for zl in range(2):
        for xx in range(4):
            for zh in range(2):
                total = wide(part[zl, xx, y, zh, :, 384:768])
                for j in range(3):
                    total += wide(first1[j, zl, xx, zh])
                mid1[zl, zh, xx] = total.astype(mid1.dtype)
    for by in (2, 1, 3):
        far = (z + by) % 4
        second(1, by, mid1.at[far % 2, far // 2], second1.at[by - 1], 2)

    for copy in waits[2]:
        copy.wait_recv()
    for xx in range(4):
        for yy in range(4):
            total = wide(part[z_lo, xx, yy, z_hi, :, 768:1024])
            for j in range(3):
                total += wide(first2[j, xx, yy])
            mid2[xx, yy] = total.astype(mid2.dtype)
    for by in (2, 1, 3):
        second(2, by, mid2.at[(x + by) % 4], second2.at[by - 1], 0)

    thirds = [[], [], []]

    def third(k, by, src, dst, axis):
        n = k * 3 + by - 1
        copy = remote(src, dst, send3.at[n], recv3.at[n], along(axis, by))
        copy.start()
        thirds[k].append(copy)

    for copy in seconds[0]:
        copy.wait_recv()
    for zl in range(2):
        for zh in range(2):
            total = wide(mid0[y, zl, zh])
            for j in range(3):
                total += wide(second0[j, zl, zh])
            late0[zl, zh] = total.astype(jnp.bfloat16)
    for by in (2, 1, 3):
        far = (z + by) % 4
        third(0, by, late0.at[far % 2, far // 2], third0.at[by - 1], 2)

    for copy in seconds[1]:
        copy.wait_recv()
    for xx in range(4):
        total = wide(mid1[z_lo, z_hi, xx])
        for j in range(3):
            total += wide(second1[j, xx])
        late1[xx] = total.astype(jnp.bfloat16)
    for by in (2, 1, 3):
        third(1, by, late1.at[(x + by) % 4], third1.at[by - 1], 0)

    for copy in seconds[2]:
        copy.wait_recv()
    for yy in range(4):
        total = wide(mid2[x, yy])
        for j in range(3):
            total += wide(second2[j, yy])
        late2[yy] = total.astype(jnp.bfloat16)
    for by in (2, 1, 3):
        third(2, by, late2.at[(y + by) % 4], third2.at[by - 1], 1)

    for k in range(3):
        for copy in thirds[k]:
            copy.wait_recv()
    def last_sum(late, slots):
        return wide(late) + wide(slots[0]) + wide(slots[1]) + wide(slots[2])

    rows[:, 0:384] = last_sum(late0[z_lo, z_hi], third0)
    rows[:, 384:768] = last_sum(late1[x], third1)
    rows[:, 768:1024] = last_sum(late2[y], third2)
    last = remote(
        rows.at[pl.ds(pl.multiple_of((1 - core) * 16, 16), 16)], rows_in, end_send, end_recv,
        chip(x, y, z, 1 - core))
    last.start()
    out[:, pl.ds(mine, half)] = rows[pl.ds(pl.multiple_of(core * 16, 16), 16), :]
    last.wait_recv()
    out[:, pl.ds(others, half)] = rows_in[...]

    for copy in direct + [half_swap]:
        copy.wait_send()
    for copy in passed:
        pl.when(jnp.logical_not(ends))(copy.wait_send)
    for copy in crossing:
        pl.when(crosses)(copy.wait_send)
    pl.when(relays)(relayed.wait_send)
    for store in stores:
        store.wait()
    for copy in swaps + waits[0] + waits[1] + waits[2] + sum(seconds, []) + sum(thirds, []) + [last]:
        copy.wait_send()


def density_call(occ_energy, vir_energy, flat):
    width, panel = flat.shape
    virtuals = vir_energy.shape[0]
    half = panel // 2
    low, full = jnp.bfloat16, jnp.float32
    dma = pltpu.SemaphoreType.DMA
    block = pltpu.VMEM((width, panel), low)
    term = pltpu.VMEM((width, panel), full)
    return pl.pallas_call(
        density_kernel,
        out_shape=(
            jax.ShapeDtypeStruct((width, panel), low),
            jax.ShapeDtypeStruct((16, panel), full),
        ),
        in_specs=[
            pl.BlockSpec(memory_space=pltpu.SMEM),
            pl.BlockSpec(memory_space=pltpu.VMEM),
            pl.BlockSpec(memory_space=pl.ANY),
        ],
        out_specs=(pl.BlockSpec(memory_space=pl.ANY), pl.BlockSpec(memory_space=pltpu.VMEM)),
        scratch_shapes=[
            block, block, block,
            pltpu.VMEM((2, width, virtuals), full),
            pltpu.VMEM((2, width, virtuals), low),
            term,
            pltpu.VMEM((virtuals, virtuals), full),
            pltpu.VMEM((width // RELAYS, panel), low),
            block,
            pltpu.VMEM((panel // TILE, TILE, width), low),
            pltpu.VMEM((panel // TILE, TILE, width), low),
            pltpu.VMEM((width, half), low),
            pltpu.VMEM((2, 4, 4, 2, 32, half), low),
            pltpu.VMEM((3, 2, 4, 2, 32, 384), low),
            pltpu.VMEM((3, 2, 4, 2, 32, 384), low),
            pltpu.VMEM((3, 4, 4, 32, 256), low),
            pltpu.VMEM((4, 2, 2, 32, 384), low),
            pltpu.VMEM((2, 2, 4, 32, 384), low),
            pltpu.VMEM((4, 4, 32, 256), low),
            pltpu.VMEM((3, 2, 2, 32, 384), low),
            pltpu.VMEM((3, 4, 32, 384), low),
            pltpu.VMEM((3, 4, 32, 256), low),
            pltpu.VMEM((2, 2, 32, 384), low),
            pltpu.VMEM((4, 32, 384), low),
            pltpu.VMEM((4, 32, 256), low),
            pltpu.VMEM((3, 32, 384), low),
            pltpu.VMEM((3, 32, 384), low),
            pltpu.VMEM((3, 32, 256), low),
            pltpu.VMEM((32, half), full),
            pltpu.VMEM((16, half), full),
            dma, dma((CHUNKS,)), dma((CHUNKS,)), dma((CHUNKS,)), dma((CHUNKS,)), dma((RELAYS,)), dma((RELAYS,)),
            dma, dma, dma, dma,
            dma((8,)), dma((8,)), dma((8,)), dma((42,)), dma((42,)),
            dma((9,)), dma((9,)), dma((9,)), dma((9,)), dma, dma,
        ],
        compiler_params=pltpu.CompilerParams(
            collective_id=0, has_side_effects=True, vmem_limit_bytes=62 * 2**20),
        name="densities",
    )(occ_energy, vir_energy.reshape(1, virtuals), flat)


def hand_over_kernel(three, two, three_out, two_out):
    three_out[...] = three[...]
    two_out[...] = two[...]


def hand_over(three, two):
    part = pl.BlockSpec((three.shape[0] // 8, three.shape[1]), lambda i: (i, 0))
    whole = pl.BlockSpec(two.shape, lambda i: (0, 0))
    return pl.pallas_call(
        hand_over_kernel,
        out_shape=(
            jax.ShapeDtypeStruct(three.shape, three.dtype),
            jax.ShapeDtypeStruct(two.shape, two.dtype),
        ),
        grid=(8,),
        in_specs=[part, whole],
        out_specs=(part, whole),
        name="hand_over",
    )(three, two)


def per_device(occ_energy, vir_energy, factors):
    orbitals, virtuals, panel = factors.shape
    flat = factors.reshape(orbitals * virtuals, panel)
    gamma_three, gamma_two = density_call(occ_energy, vir_energy, flat)
    gamma_three, gamma_two = hand_over(gamma_three, gamma_two)
    return gamma_three.reshape(orbitals, virtuals, panel), gamma_two


def solution(mesh):
    placed = (P(), P(), P(("occ", "aux"), None, None))
    return jax.shard_map(
        per_device,
        mesh=mesh,
        in_specs=placed,
        out_specs=(P(("occ", "aux"), None, None), P(("occ", "aux"), None)),
        check_vma=False,
    )
```

```python
import jax
import jax.numpy as jnp
from jax import lax
from jax.experimental import pallas as pl
from jax.experimental.pallas import tpu as pltpu
from jax.sharding import PartitionSpec as P

MESH = pl.DeviceIdType.MESH
NT = (((1,), (1,)), ((), ()))
TN = (((0,), (0,)), ((), ()))
SIZES = (64,) * 14 + (32, 32, 32, 16, 16)
STARTS = tuple(sum(SIZES[:c]) for c in range(len(SIZES)))
CHUNKS = len(SIZES)
RELAYS = 16
LAG = 3
RELAY_LAG = 5
TILE = 256
COLS = ((0, 384), (384, 384), (768, 256))
NEAR_FIRST = (2, 1, 3, 0)


def device(position):
    return (position // 2, position % 2)


def by_plane(z, values):
    return jnp.where(z == 0, values[0], jnp.where(z == 1, values[1], jnp.where(z == 2, values[2], values[3])))


def coordinates():
    occ, aux = lax.axis_index("occ"), lax.axis_index("aux")
    return (occ // 8) % 4, (occ // 2) % 4, aux * 2 + occ // 32, occ % 2


def chip(x, y, z, core):
    return ((z % 2) * 32 + x * 8 + y * 2 + core, z // 2)


def density_kernel(
    occ, vir, factors, gamma_out, out, own, near, far, ints, amps, term, base, transit,
    gamma, turned, other_turned, other_own, part,
    first0, first1, first2, mid0, mid1, mid2, second0, second1, second2,
    late0, late1, late2, third0, third1, third2, rows, rows_in,
    load_sem, near_send, near_recv, far_send, far_recv, cross_send, cross_recv,
    transit_send, transit_recv, half_send, half_recv,
    store_sem, core_send, core_recv, send1, recv1, send2, recv2, send3, recv3, end_send, end_recv,
):
    width, panel = own.shape
    virtuals = vir.shape[1]
    strip = width // RELAYS
    count = 2 * lax.axis_size("occ")
    me = lax.axis_index("occ") * 2 + lax.axis_index("aux")
    even = me % 2 == 0
    step = 1 - 2 * (me % 2)
    near_block = (me + step + count) % count
    far_block = (me - step + count) % count
    onward = (me + 2 * step + count) % count
    behind = (me - 2 * step + count) % count

    x, y, z, core = coordinates()
    column = jnp.where(z < 2, x * 4 + y, 15 - (x * 4 + y))
    ends = me % 64 == jnp.where(even, 62, 1)
    crosses = (me % 64 == 0) | (me % 64 == 63)
    direct_far = jnp.logical_not(crosses)
    relays = core == jnp.where(z < 2, 1, 0)
    relay_from = by_plane(z, (127, 63, 64, 0))
    relay_to = by_plane(z, (0, 64, 63, 127))

    def relay_of(c, plane):
        at = jnp.where(plane < 2, c * 2 + 1, (RELAYS - 1 - c) * 2)
        return ((plane % 2) * 32 + at, plane // 2)

    plane_on = by_plane(z, (3, 2, 1, 0))

    z_lo, z_hi = z % 2, z // 2
    half = panel // 2
    mine = pl.multiple_of(core * half, half)
    others = pl.multiple_of((1 - core) * half, half)
    scale = float(count * width) ** (-0.5)

    def along(axis, by):
        place = [x, y, z]
        place[axis] = (place[axis] + by) % 4
        return chip(*place, core)

    def remote(src, dst, send, recv, target):
        return pltpu.make_async_remote_copy(
            src_ref=src, dst_ref=dst, send_sem=send, recv_sem=recv,
            device_id=target, device_id_type=MESH)

    load = pltpu.make_async_copy(factors, own, load_sem)
    load.start()

    barrier = pltpu.get_barrier_semaphore()
    for other in (near_block, onward, behind):
        pl.semaphore_signal(barrier, inc=1, device_id=device(other), device_id_type=MESH)
    for axis in range(3):
        for by in (1, 2, 3):
            pl.semaphore_signal(barrier, inc=1, device_id=along(axis, by), device_id_type=MESH)
    pl.semaphore_signal(barrier, inc=1, device_id=chip(x, y, z, 1 - core), device_id_type=MESH)

    @pl.when(crosses)
    def _():
        for c in range(RELAYS):
            pl.semaphore_signal(barrier, inc=1, device_id=relay_of(c, z), device_id_type=MESH)

    @pl.when(relays)
    def _():
        pl.semaphore_signal(barrier, inc=1, device_id=device(relay_from), device_id_type=MESH)

    pl.semaphore_wait(barrier, 13 + jnp.where(crosses, RELAYS, 0) + jnp.where(relays, 1, 0))

    def span(c):
        return pl.ds(STARTS[c], SIZES[c])

    def strip_at(k):
        return pl.ds(k * strip, strip)

    direct = [
        pltpu.make_async_remote_copy(
            src_ref=factors.at[span(c)], dst_ref=near.at[span(c)],
            send_sem=near_send.at[c], recv_sem=near_recv.at[c],
            device_id=device(near_block), device_id_type=MESH)
        for c in range(CHUNKS)
    ]
    passed = [
        pltpu.make_async_remote_copy(
            src_ref=near.at[span(c)], dst_ref=far.at[span(c)],
            send_sem=far_send.at[c], recv_sem=far_recv.at[c],
            device_id=device(onward), device_id_type=MESH)
        for c in range(CHUNKS)
    ]
    crossing = [
        pltpu.make_async_remote_copy(
            src_ref=factors.at[strip_at(k)], dst_ref=transit,
            send_sem=cross_send.at[k], recv_sem=transit_recv,
            device_id=relay_of(k, plane_on), device_id_type=MESH)
        for k in range(RELAYS)
    ]
    landing = [
        pltpu.make_async_remote_copy(
            src_ref=transit, dst_ref=far.at[strip_at(k)],
            send_sem=transit_send, recv_sem=cross_recv.at[k],
            device_id=device(relay_to), device_id_type=MESH)
        for k in range(RELAYS)
    ]
    relayed = pltpu.make_async_remote_copy(
        src_ref=transit, dst_ref=far.at[pl.ds(pl.multiple_of(column * strip, strip), strip)],
        send_sem=transit_send, recv_sem=cross_recv.at[column],
        device_id=device(relay_to), device_id_type=MESH)
    for copy in direct:
        copy.start()
    half_swap = remote(factors.at[:, pl.ds(others, half)], other_own, half_send, half_recv, chip(x, y, z, 1 - core))
    half_swap.start()

    def relay(k):
        @pl.when(relays & (column == k))
        def _():
            crossing[k].wait_recv()
            relayed.start()

    row = jnp.broadcast_to(vir[...], (virtuals, virtuals))
    base[...] = row + row.T
    load.wait()

    def pair_ints(block, which, piece):
        left = piece % 2 * TILE

        @pl.loop(0, width // 512)
        def _(r):
            at = pl.ds(pl.multiple_of(r * 512, 512), 512)
            ints[which, at, left:left + TILE] = lax.dot_general(
                own[at, :], block[piece * TILE:(piece + 1) * TILE, :], NT,
                preferred_element_type=jnp.float32)

    def pair_amps(which, other, n):
        other_energy = occ[2 * other + n]
        for i in range(2):
            energy = occ[2 * me + i]
            for a in range(virtuals // TILE):
                for b in range(virtuals // TILE):
                    top, side = i * virtuals + a * TILE, i * virtuals + b * TILE
                    here = ints[which, top:top + TILE, b * TILE:(b + 1) * TILE]
                    swapped = ints[which, side:side + TILE, a * TILE:(a + 1) * TILE].T
                    gap = base[a * TILE:(a + 1) * TILE, b * TILE:(b + 1) * TILE] - energy - other_energy
                    amps[which, top:top + TILE, b * TILE:(b + 1) * TILE] = (
                        (2.0 * here - swapped) / gap).astype(jnp.bfloat16)

    def pair_term(which, block, n, first=False):
        @pl.loop(0, width // 512)
        def _(r):
            at = pl.ds(pl.multiple_of(r * 512, 512), 512)
            for c in range(0, panel, 512):
                value = jnp.dot(
                    amps[which, at, :], block[n * virtuals:(n + 1) * virtuals, c:c + 512],
                    preferred_element_type=jnp.float32)
                if not first:
                    value += term[at, c:c + 512]
                term[at, c:c + 512] = value

    def far_piece(piece):
        @pl.when(crosses)
        def _():
            for k in range(piece * 4, piece * 4 + 4):
                landing[k].wait_recv()

        pair_ints(far, 1, piece)
        if piece % 2 == 1:
            pair_amps(1, far_block, piece // 2)
        if piece == 1:
            pair_term(1, far, 0)

    def near_piece(piece):
        pair_ints(near, 0, piece)
        if piece % 2 == 1:
            pair_amps(0, near_block, piece // 2)
            pair_term(0, near, piece // 2, first=piece == 1)

    ends_of = {STARTS[c] + SIZES[c]: c for c in range(CHUNKS)}
    whole = {ends_of[(p + 1) * TILE]: p for p in range(width // TILE)}
    for c in range(CHUNKS):
        direct[c].wait_recv()
        pl.when(jnp.logical_not(ends))(passed[c].start)
        if 2 * c < RELAYS:
            pl.when(crosses)(crossing[2 * c].start)
            pl.when(crosses)(crossing[2 * c + 1].start)
        if 0 <= 2 * (c - RELAY_LAG) < RELAYS:
            relay(2 * (c - RELAY_LAG))
            relay(2 * (c - RELAY_LAG) + 1)
        if c >= LAG:
            pl.when(direct_far)(passed[c - LAG].wait_recv)
            if c - LAG in whole:
                far_piece(whole[c - LAG])
        if c in whole:
            near_piece(whole[c])
    for c in range(CHUNKS - LAG, CHUNKS):
        pl.when(direct_far)(passed[c].wait_recv)
    far_piece(3)

    tiles = [(e, d) for d in NEAR_FIRST for e in (1, 0)]
    swaps = []
    stores = []
    waits = [[], [], []]

    def columns(t):
        e, d = tiles[t]
        zl, xt = (z_lo + e) % 2, (x + d) % 4
        return zl, xt, pl.ds(pl.multiple_of((zl * 4 + xt) * TILE, TILE), TILE)

    def tile_term(t):
        _, _, at = columns(t)
        for r in range(0, width, 512):
            value = term[r:r + 512, at] + jnp.dot(
                amps[1, r:r + 512, :], far[virtuals:width, at], preferred_element_type=jnp.float32)
            value = value.astype(jnp.bfloat16)
            gamma[r:r + 512, at] = value
            turned[t, :, r:r + 512] = value.T
        store = pltpu.make_async_copy(gamma.at[:, at], gamma_out.at[:, at], store_sem.at[t])
        store.start()
        stores.append(store)
        swap = remote(turned.at[t], other_turned.at[t], core_send.at[t], core_recv.at[t], chip(x, y, z, 1 - core))
        swap.start()
        swaps.append(swap)

    def finish(t):
        e, d = tiles[t]
        zl, xt, _ = columns(t)
        swaps[t].wait_recv()
        for c in range(0, half, 512):
            total = jnp.dot(
                turned[t], own[:, pl.ds(pl.multiple_of(mine + c, 512), 512)], preferred_element_type=jnp.float32)
            total += jnp.dot(other_turned[t], other_own[:, c:c + 512], preferred_element_type=jnp.float32)
            total = (total * scale).astype(jnp.bfloat16)
            for yy in range(4):
                for cc in range(2):
                    for zh in range(2):
                        at = ((yy * 2 + cc) * 2 + zh) * 16
                        part[zl, xt, yy, zh, cc * 16:(cc + 1) * 16, c:c + 512] = total[at:at + 16, :]
        copies = []
        if d:
            cols = pl.ds(*COLS[0])
            copies.append((0, part.at[zl, xt, :, :, :, cols], first0.at[d - 1, zl], along(0, d)))
        for by in (2, 1, 3):
            cols = pl.ds(*COLS[1])
            copies.append((1, part.at[zl, xt, (y + by) % 4, :, :, cols], first1.at[by - 1, zl, xt], along(1, by)))
        for by in ((1, 3) if e else (2,)):
            cols = pl.ds(*COLS[2])
            copies.append((2, part.at[zl, xt, :, ((z + by) % 4) // 2, :, cols], first2.at[by - 1, xt], along(2, by)))
        for k, src, dst, target in copies:
            n = sum(len(w) for w in waits)
            copy = remote(src, dst, send1.at[n], recv1.at[n], target)
            copy.start()
            waits[k].append(copy)

    half_swap.wait_recv()
    for t in range(len(tiles)):
        tile_term(t)
        if t:
            finish(t - 1)
    finish(len(tiles) - 1)

    def wide(value):
        return value.astype(jnp.float32)

    seconds = [[], [], []]

    def second(k, by, src, dst, axis):
        n = k * 3 + by - 1
        copy = remote(src, dst, send2.at[n], recv2.at[n], along(axis, by))
        copy.start()
        seconds[k].append(copy)

    for copy in waits[0]:
        copy.wait_recv()
    for zl in range(2):
        for yy in range(4):
            for zh in range(2):
                total = wide(part[zl, x, yy, zh, :, 0:384])
                for j in range(3):
                    total += wide(first0[j, zl, yy, zh])
                mid0[yy, zl, zh] = total.astype(mid0.dtype)
    for by in (2, 1, 3):
        second(0, by, mid0.at[(y + by) % 4], second0.at[by - 1], 1)

    for copy in waits[1]:
        copy.wait_recv()
    for zl in range(2):
        for xx in range(4):
            for zh in range(2):
                total = wide(part[zl, xx, y, zh, :, 384:768])
                for j in range(3):
                    total += wide(first1[j, zl, xx, zh])
                mid1[zl, zh, xx] = total.astype(mid1.dtype)
    for by in (2, 1, 3):
        far = (z + by) % 4
        second(1, by, mid1.at[far % 2, far // 2], second1.at[by - 1], 2)

    for copy in waits[2]:
        copy.wait_recv()
    for xx in range(4):
        for yy in range(4):
            total = wide(part[z_lo, xx, yy, z_hi, :, 768:1024])
            for j in range(3):
                total += wide(first2[j, xx, yy])
            mid2[xx, yy] = total.astype(mid2.dtype)
    for by in (2, 1, 3):
        second(2, by, mid2.at[(x + by) % 4], second2.at[by - 1], 0)

    thirds = [[], [], []]

    def third(k, by, src, dst, axis):
        n = k * 3 + by - 1
        copy = remote(src, dst, send3.at[n], recv3.at[n], along(axis, by))
        copy.start()
        thirds[k].append(copy)

    for copy in seconds[0]:
        copy.wait_recv()
    for zl in range(2):
        for zh in range(2):
            total = wide(mid0[y, zl, zh])
            for j in range(3):
                total += wide(second0[j, zl, zh])
            late0[zl, zh] = total.astype(jnp.bfloat16)
    for by in (2, 1, 3):
        far = (z + by) % 4
        third(0, by, late0.at[far % 2, far // 2], third0.at[by - 1], 2)

    for copy in seconds[1]:
        copy.wait_recv()
    for xx in range(4):
        total = wide(mid1[z_lo, z_hi, xx])
        for j in range(3):
            total += wide(second1[j, xx])
        late1[xx] = total.astype(jnp.bfloat16)
    for by in (2, 1, 3):
        third(1, by, late1.at[(x + by) % 4], third1.at[by - 1], 0)

    for copy in seconds[2]:
        copy.wait_recv()
    for yy in range(4):
        total = wide(mid2[x, yy])
        for j in range(3):
            total += wide(second2[j, yy])
        late2[yy] = total.astype(jnp.bfloat16)
    for by in (2, 1, 3):
        third(2, by, late2.at[(y + by) % 4], third2.at[by - 1], 1)

    for k in range(3):
        for copy in thirds[k]:
            copy.wait_recv()
    def last_sum(late, slots):
        return wide(late) + wide(slots[0]) + wide(slots[1]) + wide(slots[2])

    rows[:, 0:384] = last_sum(late0[z_lo, z_hi], third0)
    rows[:, 384:768] = last_sum(late1[x], third1)
    rows[:, 768:1024] = last_sum(late2[y], third2)
    last = remote(
        rows.at[pl.ds(pl.multiple_of((1 - core) * 16, 16), 16)], rows_in, end_send, end_recv,
        chip(x, y, z, 1 - core))
    last.start()
    out[:, pl.ds(mine, half)] = rows[pl.ds(pl.multiple_of(core * 16, 16), 16), :]
    last.wait_recv()
    out[:, pl.ds(others, half)] = rows_in[...]

    for copy in direct + [half_swap]:
        copy.wait_send()
    for copy in passed:
        pl.when(jnp.logical_not(ends))(copy.wait_send)
    for copy in crossing:
        pl.when(crosses)(copy.wait_send)
    pl.when(relays)(relayed.wait_send)
    for store in stores:
        store.wait()
    for copy in swaps + waits[0] + waits[1] + waits[2] + sum(seconds, []) + sum(thirds, []) + [last]:
        copy.wait_send()


def density_call(occ_energy, vir_energy, flat):
    width, panel = flat.shape
    virtuals = vir_energy.shape[0]
    half = panel // 2
    low, full = jnp.bfloat16, jnp.float32
    dma = pltpu.SemaphoreType.DMA
    block = pltpu.VMEM((width, panel), low)
    term = pltpu.VMEM((width, panel), full)
    return pl.pallas_call(
        density_kernel,
        out_shape=(
            jax.ShapeDtypeStruct((width, panel), low),
            jax.ShapeDtypeStruct((16, panel), full),
        ),
        in_specs=[
            pl.BlockSpec(memory_space=pltpu.SMEM),
            pl.BlockSpec(memory_space=pltpu.VMEM),
            pl.BlockSpec(memory_space=pl.ANY),
        ],
        out_specs=(pl.BlockSpec(memory_space=pl.ANY), pl.BlockSpec(memory_space=pltpu.VMEM)),
        scratch_shapes=[
            block, block, block,
            pltpu.VMEM((2, width, virtuals), full),
            pltpu.VMEM((2, width, virtuals), low),
            term,
            pltpu.VMEM((virtuals, virtuals), full),
            pltpu.VMEM((width // RELAYS, panel), low),
            block,
            pltpu.VMEM((panel // TILE, TILE, width), low),
            pltpu.VMEM((panel // TILE, TILE, width), low),
            pltpu.VMEM((width, half), low),
            pltpu.VMEM((2, 4, 4, 2, 32, half), low),
            pltpu.VMEM((3, 2, 4, 2, 32, 384), low),
            pltpu.VMEM((3, 2, 4, 2, 32, 384), low),
            pltpu.VMEM((3, 4, 4, 32, 256), low),
            pltpu.VMEM((4, 2, 2, 32, 384), low),
            pltpu.VMEM((2, 2, 4, 32, 384), low),
            pltpu.VMEM((4, 4, 32, 256), low),
            pltpu.VMEM((3, 2, 2, 32, 384), low),
            pltpu.VMEM((3, 4, 32, 384), low),
            pltpu.VMEM((3, 4, 32, 256), low),
            pltpu.VMEM((2, 2, 32, 384), low),
            pltpu.VMEM((4, 32, 384), low),
            pltpu.VMEM((4, 32, 256), low),
            pltpu.VMEM((3, 32, 384), low),
            pltpu.VMEM((3, 32, 384), low),
            pltpu.VMEM((3, 32, 256), low),
            pltpu.VMEM((32, half), full),
            pltpu.VMEM((16, half), full),
            dma, dma((CHUNKS,)), dma((CHUNKS,)), dma((CHUNKS,)), dma((CHUNKS,)), dma((RELAYS,)), dma((RELAYS,)),
            dma, dma, dma, dma,
            dma((8,)), dma((8,)), dma((8,)), dma((42,)), dma((42,)),
            dma((9,)), dma((9,)), dma((9,)), dma((9,)), dma, dma,
        ],
        compiler_params=pltpu.CompilerParams(
            collective_id=0, has_side_effects=True, vmem_limit_bytes=62 * 2**20),
        name="densities",
    )(occ_energy, vir_energy.reshape(1, virtuals), flat)


def hand_over_kernel(three, two, three_out, two_out, block, small, in_sem, out_sem):
    size = block.shape[0] // 8
    pieces = [(three.at[pl.ds(p * size, size)], block.at[pl.ds(p * size, size)], three_out.at[pl.ds(p * size, size)])
              for p in range(8)]
    pieces.append((two, small, two_out))
    reads = [pltpu.make_async_copy(src, held, in_sem.at[p]) for p, (src, held, _) in enumerate(pieces)]
    writes = [pltpu.make_async_copy(held, dst, out_sem.at[p]) for p, (_, held, dst) in enumerate(pieces)]
    for copy in reads:
        copy.start()
    for read, write in zip(reads, writes):
        read.wait()
        write.start()
    for copy in writes:
        copy.wait()


def hand_over(three, two):
    anywhere = pl.BlockSpec(memory_space=pl.ANY)
    return pl.pallas_call(
        hand_over_kernel,
        out_shape=(
            jax.ShapeDtypeStruct(three.shape, three.dtype),
            jax.ShapeDtypeStruct(two.shape, two.dtype),
        ),
        in_specs=[anywhere] * 2,
        out_specs=(anywhere, anywhere),
        scratch_shapes=[
            pltpu.VMEM(three.shape, three.dtype),
            pltpu.VMEM(two.shape, two.dtype),
            pltpu.SemaphoreType.DMA((9,)),
            pltpu.SemaphoreType.DMA((9,)),
        ],
        compiler_params=pltpu.CompilerParams(vmem_limit_bytes=62 * 2**20),
        name="hand_over",
    )(three, two)


def per_device(occ_energy, vir_energy, factors):
    orbitals, virtuals, panel = factors.shape
    flat = factors.reshape(orbitals * virtuals, panel)
    gamma_three, gamma_two = density_call(occ_energy, vir_energy, flat)
    gamma_three, gamma_two = hand_over(gamma_three, gamma_two)
    return gamma_three.reshape(orbitals, virtuals, panel), gamma_two


def solution(mesh):
    placed = (P(), P(), P(("occ", "aux"), None, None))
    return jax.shard_map(
        per_device,
        mesh=mesh,
        in_specs=placed,
        out_specs=(P(("occ", "aux"), None, None), P(("occ", "aux"), None)),
        check_vma=False,
    )
```

```python
import jax
import jax.numpy as jnp
from jax import lax
from jax.experimental import pallas as pl
from jax.experimental.pallas import tpu as pltpu
from jax.sharding import PartitionSpec as P

MESH = pl.DeviceIdType.MESH
NT = (((1,), (1,)), ((), ()))
TN = (((0,), (0,)), ((), ()))
SIZES = (64,) * 14 + (32, 32, 32, 16, 16)
STARTS = tuple(sum(SIZES[:c]) for c in range(len(SIZES)))
CHUNKS = len(SIZES)
RELAYS = 16
LAG = 5
RELAY_LAG = 5
TILE = 256
COLS = ((0, 384), (384, 384), (768, 256))
NEAR_FIRST = (2, 1, 3, 0)


def device(position):
    return (position // 2, position % 2)


def by_plane(z, values):
    return jnp.where(z == 0, values[0], jnp.where(z == 1, values[1], jnp.where(z == 2, values[2], values[3])))


def coordinates():
    occ, aux = lax.axis_index("occ"), lax.axis_index("aux")
    return (occ // 8) % 4, (occ // 2) % 4, aux * 2 + occ // 32, occ % 2


def chip(x, y, z, core):
    return ((z % 2) * 32 + x * 8 + y * 2 + core, z // 2)


def density_kernel(
    occ, vir, factors, gamma_out, out, own, near, far, ints, amps, term, base, transit,
    gamma, turned, other_turned, other_own, part,
    first0, first1, first2, mid0, mid1, mid2, second0, second1, second2,
    late0, late1, late2, third0, third1, third2, rows, rows_in,
    load_sem, near_send, near_recv, far_send, far_recv, cross_send, cross_recv,
    transit_send, transit_recv, half_send, half_recv,
    store_sem, core_send, core_recv, send1, recv1, send2, recv2, send3, recv3, end_send, end_recv,
):
    width, panel = own.shape
    virtuals = vir.shape[1]
    strip = width // RELAYS
    count = 2 * lax.axis_size("occ")
    me = lax.axis_index("occ") * 2 + lax.axis_index("aux")
    even = me % 2 == 0
    step = 1 - 2 * (me % 2)
    near_block = (me + step + count) % count
    far_block = (me - step + count) % count
    onward = (me + 2 * step + count) % count
    behind = (me - 2 * step + count) % count

    x, y, z, core = coordinates()
    column = jnp.where(z < 2, x * 4 + y, 15 - (x * 4 + y))
    ends = me % 64 == jnp.where(even, 62, 1)
    crosses = (me % 64 == 0) | (me % 64 == 63)
    direct_far = jnp.logical_not(crosses)
    relays = core == jnp.where(z < 2, 1, 0)
    relay_from = by_plane(z, (127, 63, 64, 0))
    relay_to = by_plane(z, (0, 64, 63, 127))

    def relay_of(c, plane):
        at = jnp.where(plane < 2, c * 2 + 1, (RELAYS - 1 - c) * 2)
        return ((plane % 2) * 32 + at, plane // 2)

    plane_on = by_plane(z, (3, 2, 1, 0))

    z_lo, z_hi = z % 2, z // 2
    half = panel // 2
    mine = pl.multiple_of(core * half, half)
    others = pl.multiple_of((1 - core) * half, half)
    scale = float(count * width) ** (-0.5)

    def along(axis, by):
        place = [x, y, z]
        place[axis] = (place[axis] + by) % 4
        return chip(*place, core)

    def remote(src, dst, send, recv, target):
        return pltpu.make_async_remote_copy(
            src_ref=src, dst_ref=dst, send_sem=send, recv_sem=recv,
            device_id=target, device_id_type=MESH)

    load = pltpu.make_async_copy(factors, own, load_sem)
    load.start()

    barrier = pltpu.get_barrier_semaphore()
    for other in (near_block, onward, behind):
        pl.semaphore_signal(barrier, inc=1, device_id=device(other), device_id_type=MESH)
    for axis in range(3):
        for by in (1, 2, 3):
            pl.semaphore_signal(barrier, inc=1, device_id=along(axis, by), device_id_type=MESH)
    pl.semaphore_signal(barrier, inc=1, device_id=chip(x, y, z, 1 - core), device_id_type=MESH)

    @pl.when(crosses)
    def _():
        for c in range(RELAYS):
            pl.semaphore_signal(barrier, inc=1, device_id=relay_of(c, z), device_id_type=MESH)

    @pl.when(relays)
    def _():
        pl.semaphore_signal(barrier, inc=1, device_id=device(relay_from), device_id_type=MESH)

    pl.semaphore_wait(barrier, 13 + jnp.where(crosses, RELAYS, 0) + jnp.where(relays, 1, 0))

    def span(c):
        return pl.ds(STARTS[c], SIZES[c])

    def strip_at(k):
        return pl.ds(k * strip, strip)

    direct = [
        pltpu.make_async_remote_copy(
            src_ref=factors.at[span(c)], dst_ref=near.at[span(c)],
            send_sem=near_send.at[c], recv_sem=near_recv.at[c],
            device_id=device(near_block), device_id_type=MESH)
        for c in range(CHUNKS)
    ]
    passed = [
        pltpu.make_async_remote_copy(
            src_ref=near.at[span(c)], dst_ref=far.at[span(c)],
            send_sem=far_send.at[c], recv_sem=far_recv.at[c],
            device_id=device(onward), device_id_type=MESH)
        for c in range(CHUNKS)
    ]
    crossing = [
        pltpu.make_async_remote_copy(
            src_ref=factors.at[strip_at(k)], dst_ref=transit,
            send_sem=cross_send.at[k], recv_sem=transit_recv,
            device_id=relay_of(k, plane_on), device_id_type=MESH)
        for k in range(RELAYS)
    ]
    landing = [
        pltpu.make_async_remote_copy(
            src_ref=transit, dst_ref=far.at[strip_at(k)],
            send_sem=transit_send, recv_sem=cross_recv.at[k],
            device_id=device(relay_to), device_id_type=MESH)
        for k in range(RELAYS)
    ]
    relayed = pltpu.make_async_remote_copy(
        src_ref=transit, dst_ref=far.at[pl.ds(pl.multiple_of(column * strip, strip), strip)],
        send_sem=transit_send, recv_sem=cross_recv.at[column],
        device_id=device(relay_to), device_id_type=MESH)
    for copy in direct:
        copy.start()
    half_swap = remote(factors.at[:, pl.ds(others, half)], other_own, half_send, half_recv, chip(x, y, z, 1 - core))
    half_swap.start()

    def relay(k):
        @pl.when(relays & (column == k))
        def _():
            crossing[k].wait_recv()
            relayed.start()

    row = jnp.broadcast_to(vir[...], (virtuals, virtuals))
    base[...] = row + row.T
    load.wait()

    def pair_ints(block, which, piece):
        left = piece % 2 * TILE

        @pl.loop(0, width // 512)
        def _(r):
            at = pl.ds(pl.multiple_of(r * 512, 512), 512)
            ints[which, at, left:left + TILE] = lax.dot_general(
                own[at, :], block[piece * TILE:(piece + 1) * TILE, :], NT,
                preferred_element_type=jnp.float32)

    def pair_amps(which, other, n):
        other_energy = occ[2 * other + n]
        for i in range(2):
            energy = occ[2 * me + i]
            for a in range(virtuals // TILE):
                for b in range(virtuals // TILE):
                    top, side = i * virtuals + a * TILE, i * virtuals + b * TILE
                    here = ints[which, top:top + TILE, b * TILE:(b + 1) * TILE]
                    swapped = ints[which, side:side + TILE, a * TILE:(a + 1) * TILE].T
                    gap = base[a * TILE:(a + 1) * TILE, b * TILE:(b + 1) * TILE] - energy - other_energy
                    amps[which, top:top + TILE, b * TILE:(b + 1) * TILE] = (
                        (2.0 * here - swapped) / gap).astype(jnp.bfloat16)

    def pair_term(which, block, n, first=False):
        @pl.loop(0, width // 512)
        def _(r):
            at = pl.ds(pl.multiple_of(r * 512, 512), 512)
            for c in range(0, panel, 512):
                value = jnp.dot(
                    amps[which, at, :], block[n * virtuals:(n + 1) * virtuals, c:c + 512],
                    preferred_element_type=jnp.float32)
                if not first:
                    value += term[at, c:c + 512]
                term[at, c:c + 512] = value

    def far_piece(piece):
        @pl.when(crosses)
        def _():
            for k in range(piece * 4, piece * 4 + 4):
                landing[k].wait_recv()

        pair_ints(far, 1, piece)
        if piece % 2 == 1:
            pair_amps(1, far_block, piece // 2)
        if piece == 1:
            pair_term(1, far, 0)

    def near_piece(piece):
        pair_ints(near, 0, piece)
        if piece % 2 == 1:
            pair_amps(0, near_block, piece // 2)
            pair_term(0, near, piece // 2, first=piece == 1)

    ends_of = {STARTS[c] + SIZES[c]: c for c in range(CHUNKS)}
    whole = {ends_of[(p + 1) * TILE]: p for p in range(width // TILE)}
    for c in range(CHUNKS):
        direct[c].wait_recv()
        pl.when(jnp.logical_not(ends))(passed[c].start)
        if 2 * c < RELAYS:
            pl.when(crosses)(crossing[2 * c].start)
            pl.when(crosses)(crossing[2 * c + 1].start)
        if 0 <= 2 * (c - RELAY_LAG) < RELAYS:
            relay(2 * (c - RELAY_LAG))
            relay(2 * (c - RELAY_LAG) + 1)
        if c >= LAG:
            pl.when(direct_far)(passed[c - LAG].wait_recv)
            if c - LAG in whole:
                far_piece(whole[c - LAG])
        if c in whole:
            near_piece(whole[c])
    for c in range(CHUNKS - LAG, CHUNKS):
        pl.when(direct_far)(passed[c].wait_recv)
    far_piece(3)

    tiles = [(e, d) for d in NEAR_FIRST for e in (1, 0)]
    swaps = []
    stores = []
    waits = [[], [], []]

    def columns(t):
        e, d = tiles[t]
        zl, xt = (z_lo + e) % 2, (x + d) % 4
        return zl, xt, pl.ds(pl.multiple_of((zl * 4 + xt) * TILE, TILE), TILE)

    def tile_term(t):
        _, _, at = columns(t)
        for r in range(0, width, 512):
            value = term[r:r + 512, at] + jnp.dot(
                amps[1, r:r + 512, :], far[virtuals:width, at], preferred_element_type=jnp.float32)
            value = value.astype(jnp.bfloat16)
            gamma[r:r + 512, at] = value
            turned[t, :, r:r + 512] = value.T
        store = pltpu.make_async_copy(gamma.at[:, at], gamma_out.at[:, at], store_sem.at[t])
        store.start()
        stores.append(store)
        swap = remote(turned.at[t], other_turned.at[t], core_send.at[t], core_recv.at[t], chip(x, y, z, 1 - core))
        swap.start()
        swaps.append(swap)

    def finish(t):
        e, d = tiles[t]
        zl, xt, _ = columns(t)
        swaps[t].wait_recv()
        for c in range(0, half, 512):
            total = jnp.dot(
                turned[t], own[:, pl.ds(pl.multiple_of(mine + c, 512), 512)], preferred_element_type=jnp.float32)
            total += jnp.dot(other_turned[t], other_own[:, c:c + 512], preferred_element_type=jnp.float32)
            total = (total * scale).astype(jnp.bfloat16)
            for yy in range(4):
                for cc in range(2):
                    for zh in range(2):
                        at = ((yy * 2 + cc) * 2 + zh) * 16
                        part[zl, xt, yy, zh, cc * 16:(cc + 1) * 16, c:c + 512] = total[at:at + 16, :]
        copies = []
        if d:
            cols = pl.ds(*COLS[0])
            copies.append((0, part.at[zl, xt, :, :, :, cols], first0.at[d - 1, zl], along(0, d)))
        for by in (2, 1, 3):
            cols = pl.ds(*COLS[1])
            copies.append((1, part.at[zl, xt, (y + by) % 4, :, :, cols], first1.at[by - 1, zl, xt], along(1, by)))
        for by in ((1, 3) if e else (2,)):
            cols = pl.ds(*COLS[2])
            copies.append((2, part.at[zl, xt, :, ((z + by) % 4) // 2, :, cols], first2.at[by - 1, xt], along(2, by)))
        for k, src, dst, target in copies:
            n = sum(len(w) for w in waits)
            copy = remote(src, dst, send1.at[n], recv1.at[n], target)
            copy.start()
            waits[k].append(copy)

    half_swap.wait_recv()
    for t in range(len(tiles)):
        tile_term(t)
        if t:
            finish(t - 1)
    finish(len(tiles) - 1)

    def wide(value):
        return value.astype(jnp.float32)

    seconds = [[], [], []]

    def second(k, by, src, dst, axis):
        n = k * 3 + by - 1
        copy = remote(src, dst, send2.at[n], recv2.at[n], along(axis, by))
        copy.start()
        seconds[k].append(copy)

    for copy in waits[0]:
        copy.wait_recv()
    for zl in range(2):
        for yy in range(4):
            for zh in range(2):
                total = wide(part[zl, x, yy, zh, :, 0:384])
                for j in range(3):
                    total += wide(first0[j, zl, yy, zh])
                mid0[yy, zl, zh] = total.astype(mid0.dtype)
    for by in (2, 1, 3):
        second(0, by, mid0.at[(y + by) % 4], second0.at[by - 1], 1)

    for copy in waits[1]:
        copy.wait_recv()
    for zl in range(2):
        for xx in range(4):
            for zh in range(2):
                total = wide(part[zl, xx, y, zh, :, 384:768])
                for j in range(3):
                    total += wide(first1[j, zl, xx, zh])
                mid1[zl, zh, xx] = total.astype(mid1.dtype)
    for by in (2, 1, 3):
        far = (z + by) % 4
        second(1, by, mid1.at[far % 2, far // 2], second1.at[by - 1], 2)

    for copy in waits[2]:
        copy.wait_recv()
    for xx in range(4):
        for yy in range(4):
            total = wide(part[z_lo, xx, yy, z_hi, :, 768:1024])
            for j in range(3):
                total += wide(first2[j, xx, yy])
            mid2[xx, yy] = total.astype(mid2.dtype)
    for by in (2, 1, 3):
        second(2, by, mid2.at[(x + by) % 4], second2.at[by - 1], 0)

    thirds = [[], [], []]

    def third(k, by, src, dst, axis):
        n = k * 3 + by - 1
        copy = remote(src, dst, send3.at[n], recv3.at[n], along(axis, by))
        copy.start()
        thirds[k].append(copy)

    for copy in seconds[0]:
        copy.wait_recv()
    for zl in range(2):
        for zh in range(2):
            total = wide(mid0[y, zl, zh])
            for j in range(3):
                total += wide(second0[j, zl, zh])
            late0[zl, zh] = total.astype(jnp.bfloat16)
    for by in (2, 1, 3):
        far = (z + by) % 4
        third(0, by, late0.at[far % 2, far // 2], third0.at[by - 1], 2)

    for copy in seconds[1]:
        copy.wait_recv()
    for xx in range(4):
        total = wide(mid1[z_lo, z_hi, xx])
        for j in range(3):
            total += wide(second1[j, xx])
        late1[xx] = total.astype(jnp.bfloat16)
    for by in (2, 1, 3):
        third(1, by, late1.at[(x + by) % 4], third1.at[by - 1], 0)

    for copy in seconds[2]:
        copy.wait_recv()
    for yy in range(4):
        total = wide(mid2[x, yy])
        for j in range(3):
            total += wide(second2[j, yy])
        late2[yy] = total.astype(jnp.bfloat16)
    for by in (2, 1, 3):
        third(2, by, late2.at[(y + by) % 4], third2.at[by - 1], 1)

    for k in range(3):
        for copy in thirds[k]:
            copy.wait_recv()
    def last_sum(late, slots):
        return wide(late) + wide(slots[0]) + wide(slots[1]) + wide(slots[2])

    rows[:, 0:384] = last_sum(late0[z_lo, z_hi], third0)
    rows[:, 384:768] = last_sum(late1[x], third1)
    rows[:, 768:1024] = last_sum(late2[y], third2)
    last = remote(
        rows.at[pl.ds(pl.multiple_of((1 - core) * 16, 16), 16)], rows_in, end_send, end_recv,
        chip(x, y, z, 1 - core))
    last.start()
    out[:, pl.ds(mine, half)] = rows[pl.ds(pl.multiple_of(core * 16, 16), 16), :]
    last.wait_recv()
    out[:, pl.ds(others, half)] = rows_in[...]

    for copy in direct + [half_swap]:
        copy.wait_send()
    for copy in passed:
        pl.when(jnp.logical_not(ends))(copy.wait_send)
    for copy in crossing:
        pl.when(crosses)(copy.wait_send)
    pl.when(relays)(relayed.wait_send)
    for store in stores:
        store.wait()
    for copy in swaps + waits[0] + waits[1] + waits[2] + sum(seconds, []) + sum(thirds, []) + [last]:
        copy.wait_send()


def density_call(occ_energy, vir_energy, flat):
    width, panel = flat.shape
    virtuals = vir_energy.shape[0]
    half = panel // 2
    low, full = jnp.bfloat16, jnp.float32
    dma = pltpu.SemaphoreType.DMA
    block = pltpu.VMEM((width, panel), low)
    term = pltpu.VMEM((width, panel), full)
    return pl.pallas_call(
        density_kernel,
        out_shape=(
            jax.ShapeDtypeStruct((width, panel), low),
            jax.ShapeDtypeStruct((16, panel), full),
        ),
        in_specs=[
            pl.BlockSpec(memory_space=pltpu.SMEM),
            pl.BlockSpec(memory_space=pltpu.VMEM),
            pl.BlockSpec(memory_space=pl.ANY),
        ],
        out_specs=(pl.BlockSpec(memory_space=pl.ANY), pl.BlockSpec(memory_space=pltpu.VMEM)),
        scratch_shapes=[
            block, block, block,
            pltpu.VMEM((2, width, virtuals), full),
            pltpu.VMEM((2, width, virtuals), low),
            term,
            pltpu.VMEM((virtuals, virtuals), full),
            pltpu.VMEM((width // RELAYS, panel), low),
            block,
            pltpu.VMEM((panel // TILE, TILE, width), low),
            pltpu.VMEM((panel // TILE, TILE, width), low),
            pltpu.VMEM((width, half), low),
            pltpu.VMEM((2, 4, 4, 2, 32, half), low),
            pltpu.VMEM((3, 2, 4, 2, 32, 384), low),
            pltpu.VMEM((3, 2, 4, 2, 32, 384), low),
            pltpu.VMEM((3, 4, 4, 32, 256), low),
            pltpu.VMEM((4, 2, 2, 32, 384), low),
            pltpu.VMEM((2, 2, 4, 32, 384), low),
            pltpu.VMEM((4, 4, 32, 256), low),
            pltpu.VMEM((3, 2, 2, 32, 384), low),
            pltpu.VMEM((3, 4, 32, 384), low),
            pltpu.VMEM((3, 4, 32, 256), low),
            pltpu.VMEM((2, 2, 32, 384), low),
            pltpu.VMEM((4, 32, 384), low),
            pltpu.VMEM((4, 32, 256), low),
            pltpu.VMEM((3, 32, 384), low),
            pltpu.VMEM((3, 32, 384), low),
            pltpu.VMEM((3, 32, 256), low),
            pltpu.VMEM((32, half), full),
            pltpu.VMEM((16, half), full),
            dma, dma((CHUNKS,)), dma((CHUNKS,)), dma((CHUNKS,)), dma((CHUNKS,)), dma((RELAYS,)), dma((RELAYS,)),
            dma, dma, dma, dma,
            dma((8,)), dma((8,)), dma((8,)), dma((42,)), dma((42,)),
            dma((9,)), dma((9,)), dma((9,)), dma((9,)), dma, dma,
        ],
        compiler_params=pltpu.CompilerParams(
            collective_id=0, has_side_effects=True, vmem_limit_bytes=62 * 2**20),
        name="densities",
    )(occ_energy, vir_energy.reshape(1, virtuals), flat)


def hand_over_kernel(three, two, three_out, two_out, block, small, in_sem, out_sem):
    size = block.shape[0] // 8
    pieces = [(three.at[pl.ds(p * size, size)], block.at[pl.ds(p * size, size)], three_out.at[pl.ds(p * size, size)])
              for p in range(8)]
    pieces.append((two, small, two_out))
    reads = [pltpu.make_async_copy(src, held, in_sem.at[p]) for p, (src, held, _) in enumerate(pieces)]
    writes = [pltpu.make_async_copy(held, dst, out_sem.at[p]) for p, (_, held, dst) in enumerate(pieces)]
    for copy in reads:
        copy.start()
    for read, write in zip(reads, writes):
        read.wait()
        write.start()
    for copy in writes:
        copy.wait()


def hand_over(three, two):
    anywhere = pl.BlockSpec(memory_space=pl.ANY)
    return pl.pallas_call(
        hand_over_kernel,
        out_shape=(
            jax.ShapeDtypeStruct(three.shape, three.dtype),
            jax.ShapeDtypeStruct(two.shape, two.dtype),
        ),
        in_specs=[anywhere] * 2,
        out_specs=(anywhere, anywhere),
        scratch_shapes=[
            pltpu.VMEM(three.shape, three.dtype),
            pltpu.VMEM(two.shape, two.dtype),
            pltpu.SemaphoreType.DMA((9,)),
            pltpu.SemaphoreType.DMA((9,)),
        ],
        compiler_params=pltpu.CompilerParams(vmem_limit_bytes=62 * 2**20),
        name="hand_over",
    )(three, two)


def per_device(occ_energy, vir_energy, factors):
    orbitals, virtuals, panel = factors.shape
    flat = factors.reshape(orbitals * virtuals, panel)
    gamma_three, gamma_two = density_call(occ_energy, vir_energy, flat)
    gamma_three, gamma_two = hand_over(gamma_three, gamma_two)
    return gamma_three.reshape(orbitals, virtuals, panel), gamma_two


def solution(mesh):
    placed = (P(), P(), P(("occ", "aux"), None, None))
    return jax.shard_map(
        per_device,
        mesh=mesh,
        in_specs=placed,
        out_specs=(P(("occ", "aux"), None, None), P(("occ", "aux"), None)),
        check_vma=False,
    )
```
